32 devices in a mesh: narrow: 4 (over y, x), wide: 8 (over z, core).
Axes of the slice: x: 2, y: 2, z: 4, core: 2. Of those that a mesh axis runs over, the one named last changes fastest.
Arguments:
- hidden_in: bfloat16 [16, 2048, 768], P('wide', 'narrow'), may hold values from -6 to 6
- lengths: int32 [16], P('wide'), may hold values from 512 to 2048, as said below
- routes: int32 [16, 2048, 1], P('wide', 'narrow'), may hold values from 0 to 15
- norm_gain_attn: float32 [768], replicated, may hold values from 0.5 to 1.5
- query_weight: bfloat16 [768, 768], replicated, may hold values from -0.21875 to 0.21875
- key_weight: bfloat16 [768, 768], replicated, may hold values from -0.21875 to 0.21875
- value_weight: bfloat16 [768, 768], replicated, may hold values from -0.21875 to 0.21875
- out_weight: bfloat16 [768, 768], replicated, may hold values from -0.875 to 0.875
- bias_table: float32 [32, 12], replicated, may hold values from -4 to 4
- norm_gain_ffn: float32 [768], replicated, may hold values from 0.5 to 1.5
- router_weight: bfloat16 [768, 16], replicated, may hold values from -0.109375 to 0.109375
- expert_in: bfloat16 [16, 768, 3072], P('wide', None, 'narrow'), may hold values from -0.21875 to 0.21875
- expert_out: bfloat16 [16, 3072, 768], P('wide', 'narrow'), may hold values from -6 to 6
- cotangent: bfloat16 [16, 2048, 768], P('wide', 'narrow'), may hold values from -6 to 6
Outputs:
- block_out: float32 [16, 2048, 768], P('wide', 'narrow')
- grad_hidden: float32 [16, 2048, 768], P('wide', 'narrow')
- grad_gain_attn: float32 [768], replicated
- grad_query: float32 [768, 768], replicated
- grad_key: float32 [768, 768], replicated
- grad_value: float32 [768, 768], replicated
- grad_out: float32 [768, 768], replicated
- grad_table: float32 [32, 12], replicated
- grad_gain_ffn: float32 [768], replicated
- grad_router: float32 [768, 16], replicated
- grad_expert_in: float32 [16, 768, 3072], P('wide', None, 'narrow')
- grad_expert_out: float32 [16, 3072, 768], P('wide', 'narrow')
The draws below stay inside these ranges and needn't reach their ends.
Inputs may be any that keep to these rules, and one draw needn't show every extreme that they name: `lengths`: each length lies between 512 and 2048; in every aligned block of 2 sequences one has exactly 2048.
All inputs are finite; a program needn't handle non-finite values.
Results may differ from the reference program's by a relative error of at most 0.015.
Values may be sent and summed in bfloat16 or wider, within the bound.
No kernel may reach another device: no remote copies, remote signals or barrier semaphores. Data moves between devices by JAX's collectives and lax.ppermute only.
A program may use at most 448 MiB of HBM per device.

```python
import jax
import jax.numpy as jnp
from jax import lax

D = 768
HEADS = 12
HEAD_DIM = 64
FF = 3072
BUCKETS = 32
SPAN = 512
SEQ_GRP = 2
LENGTH = 2048
SEQS = 16
EXPERTS = 16
CAP = 80
N_NARROW = 4
N_WIDE = 8


def draw_lengths(key, part):
    key = jax.random.fold_in(key, 11)
    key_one, key_two = jax.random.split(key)
    ragged = jax.random.randint(key_one, (SEQS,), LENGTH // 4, LENGTH + 1)
    chosen = jax.random.randint(key_two, (SEQS // SEQ_GRP, 1), 0, SEQ_GRP)
    member = (jnp.arange(SEQ_GRP)[None, :] == chosen).reshape(SEQS)
    return jnp.where(member, LENGTH, ragged).astype(jnp.int32)


def shard_levels(rng, dims, cuts, smallest, largest):
    factor_of, own = 1.0, jax.random.fold_in(rng, 6)
    for dim, blocks in cuts:
        steps = jnp.exp(jax.random.uniform(jax.random.fold_in(own, dim), (blocks,), jnp.float32, smallest / len(cuts), largest / len(cuts)))
        factor_of = factor_of * jnp.repeat(steps, dims[dim] // blocks).reshape([-1 if axis == dim else 1 for axis in range(len(dims))])
    return factor_of


def picks_of(rng, rows, number_of, top, lift):
    sequence = jax.random.permutation(jax.random.fold_in(rng, 1), number_of)
    pull = sequence
    for power in range(3):
        pull = pull * pull // number_of
    pull = pull * lift // number_of
    chance = jax.random.randint(jax.random.fold_in(rng, 2), (rows, number_of), 0, 4096) + pull
    holders = jax.random.permutation(jax.random.fold_in(rng, 3), rows)[jnp.arange(number_of) % rows]
    chance = jnp.where(jnp.arange(rows)[:, None] == holders[None, :], 1 << 14, chance)
    priority = chance * number_of + jnp.arange(number_of)
    return lax.top_k(priority.astype(jnp.int32), top)[1].astype(jnp.int32)


def scatter_about(own_key, dims, scale, most, shards=(), kind=jnp.bfloat16):
    values = jax.random.normal(own_key, dims, jnp.float32) * scale
    if len(shards) > 0:
        values = shard_levels(own_key, dims, shards, -0.22, 0.18) * values
    return jnp.clip(values, min=-most, max=most).astype(kind)


def setup_inputs(seed: int = 0) -> dict:
    seeds = jax.random.split(jax.random.key(seed), 15)
    return {
        "hidden_in": scatter_about(seeds[0], (SEQS, LENGTH, D), 1.0, 6.0, ((0, 8), (1, 4))),
        "lengths": draw_lengths(jax.random.fold_in(seeds[14], 71), 0),
        "routes": picks_of(seeds[2], SEQS * LENGTH, EXPERTS, 1, 512).reshape((SEQS, LENGTH, 1)),
        "norm_gain_attn": jnp.clip(1.0 + 0.1 * jax.random.normal(seeds[3], (D,), jnp.float32), 0.5, 1.5),
        "query_weight": scatter_about(seeds[4], (D, D), D ** -0.5, 0.21875),
        "key_weight": scatter_about(seeds[5], (D, D), D ** -0.5, 0.21875),
        "value_weight": scatter_about(seeds[6], (D, D), D ** -0.5, 0.21875),
        "out_weight": scatter_about(seeds[7], (D, D), (D // 16) ** -0.5, 0.875),
        "bias_table": scatter_about(seeds[8], (BUCKETS, HEADS), 1.0, 4.0, (), jnp.float32),
        "norm_gain_ffn": jnp.clip(1.0 + 0.1 * jax.random.normal(seeds[9], (D,), jnp.float32), 0.5, 1.5),
        "router_weight": scatter_about(seeds[10], (D, EXPERTS), (4 * D) ** -0.5, 0.109375),
        "expert_in": scatter_about(seeds[11], (EXPERTS, D, FF), D ** -0.5, 0.21875, ((0, 8), (2, 4))),
        "expert_out": scatter_about(seeds[12], (EXPERTS, FF, D), (EXPERTS * 0.025), 6.0, ((0, 8), (1, 4))),
        "cotangent": scatter_about(seeds[13], (SEQS, LENGTH, D), 1.0, 6.0, ((0, 8), (1, 4))),
    }


epsilon = 1e-06
masked_score = -1000000000.0
bucket_edges = (1, 2, 3, 4, 5, 6, 7, 8, 12, 16, 23, 32, 46, 64, 91)
highest = lax.Precision.HIGHEST

@jax.custom_vjp
def low(v):
    return lax.optimization_barrier(v.astype(jnp.bfloat16)).astype(jnp.float32)

@jax.custom_vjp
def low_back(v):
    return v

def low_keep(v):
    return (low(v), None)

def low_pass(kept, grad):
    return (grad,)

def back_keep(v):
    return (v, None)

def back_low(kept, grad):
    return (low(grad),)
low.defvjp(low_keep, low_pass)
low_back.defvjp(back_keep, back_low)

def rms_norm(values, gain_vector):
    factor = lax.rsqrt(lax.optimization_barrier(jnp.mean(values * values, axis=-1, keepdims=True)) + epsilon)
    return values * factor * gain_vector

def bucket_of(offsets):
    magnitude = jnp.abs(offsets)
    bucket = jnp.zeros_like(offsets)
    for border in bucket_edges:
        bucket = bucket + (magnitude >= border).astype(jnp.int32)
    return bucket

def offset_bias(bias_rows, length):
    offsets = jnp.arange(2 * length - 1, dtype=jnp.int32) - (length - 1)
    half_count = bias_rows.shape[0] // 2
    bucket = bucket_of(offsets) + half_count * (offsets > 0).astype(jnp.int32)
    onehot_rows = (bucket[:, None] == jnp.arange(bias_rows.shape[0], dtype=jnp.int32)[None, :]).astype(jnp.float32)
    return jnp.dot(onehot_rows, bias_rows, precision=highest).T

def to_devices(values):
    shaped = values.reshape((N_WIDE, SEQ_GRP, N_NARROW, SPAN) + values.shape[2:])
    axis_order = (0, 2, 1, 3) + tuple(range(4, shaped.ndim))
    return jnp.transpose(shaped, axis_order).reshape((N_WIDE, N_NARROW, SEQ_GRP * SPAN) + values.shape[2:])

def from_devices(values):
    shaped = values.reshape((N_WIDE, N_NARROW, SEQ_GRP, SPAN) + values.shape[3:])
    axis_order = (0, 2, 1, 3) + tuple(range(4, shaped.ndim))
    return jnp.transpose(shaped, axis_order).reshape((SEQS, LENGTH) + values.shape[3:])

def attend_one(inputs, relative):
    query_heads, key_heads, value_heads, length_one = inputs
    positions = jnp.arange(LENGTH, dtype=jnp.int32)
    offset_index = positions[None, :] - positions[:, None] + (LENGTH - 1)
    scores = jnp.einsum('qhd,khd->hqk', query_heads, key_heads, precision=highest) * 0.125
    scores = scores + jnp.take(relative, offset_index, axis=1)
    usable = (positions < length_one)[None, None, :]
    scores = low_back(jnp.where(usable, scores, masked_score))
    row_max = lax.optimization_barrier(jnp.max(scores, axis=-1, keepdims=True))
    weights = jnp.where(usable, jnp.exp(scores - row_max), 0.0)
    attn_probs = low(weights / lax.optimization_barrier(jnp.sum(weights, axis=-1, keepdims=True)))
    return jnp.einsum('hqk,khd->qhd', attn_probs, value_heads, precision=highest)

def expert_apply(inputs):
    rows_in, weight_in, weight_out = inputs
    pre_act = low_back(jnp.dot(rows_in, weight_in, precision=highest))
    hidden = low(jax.nn.gelu(pre_act, approximate=False))
    return low_back(low(jnp.dot(hidden, weight_out, precision=highest)))

def forward(hidden_in, norm_gain_attn, query_weight, key_weight, value_weight, out_weight, bias_table, norm_gain_ffn, router_weight, expert_in, expert_out, lengths, slot_index, kept_mask, chosen):
    normed = low(rms_norm(hidden_in, norm_gain_attn))
    head_shape = (SEQS, LENGTH, HEADS, HEAD_DIM)
    queries = low_back(low(jnp.dot(normed, query_weight, precision=highest))).reshape(head_shape)
    key_rows = low_back(low(jnp.dot(normed, key_weight, precision=highest))).reshape(head_shape)
    value_rows = low_back(low(jnp.dot(normed, value_weight, precision=highest))).reshape(head_shape)
    relative = offset_bias(bias_table, LENGTH)
    attended = lax.map(jax.checkpoint(lambda inputs: attend_one(inputs, relative)), (queries, key_rows, value_rows, lengths))
    attended = low_back(low(attended.reshape(SEQS, LENGTH, D)))
    branch = low_back(jnp.dot(attended, out_weight, precision=highest))
    residual = hidden_in + branch
    ffn_input = low(rms_norm(residual, norm_gain_ffn))
    logits = low_back(jnp.dot(ffn_input, router_weight, precision=highest))
    router_probs = jax.nn.softmax(logits, axis=-1)
    gate_value = lax.optimization_barrier(jnp.sum(router_probs * chosen, axis=-1))
    slot_total = EXPERTS * N_NARROW * N_WIDE * CAP
    flat_slots = slot_index.reshape(-1)
    buffer = jnp.zeros((slot_total + 1, D), jnp.float32).at[flat_slots].add(ffn_input.reshape(-1, D))
    buffer = low_back(buffer[:slot_total].reshape(EXPERTS, slot_total // EXPERTS, D))
    results = lax.map(jax.checkpoint(expert_apply), (buffer, expert_in, expert_out))
    results = jnp.concatenate((results.reshape(slot_total, D), jnp.zeros((1, D), jnp.float32)), axis=0)
    gathered = jnp.take(results, flat_slots, axis=0).reshape(SEQS, LENGTH, D)
    return residual + (gate_value * kept_mask)[..., None] * gathered

def reference(hidden_in, lengths, routes, norm_gain_attn, query_weight, key_weight, value_weight, out_weight, bias_table, norm_gain_ffn, router_weight, expert_in, expert_out, cotangent):
    positions = jnp.arange(LENGTH, dtype=jnp.int32)
    live_bool = positions[None, :] < lengths[:, None]
    route_ids = routes[..., 0].astype(jnp.int32)
    chosen_int = ((route_ids[..., None] == jnp.arange(EXPERTS, dtype=jnp.int32)) & live_bool[..., None]).astype(jnp.int32)
    chosen_dev = to_devices(chosen_int)
    running = jnp.cumsum(chosen_dev, axis=2).astype(jnp.int32) - chosen_dev
    place_index = lax.optimization_barrier(jnp.sum(running * chosen_dev, axis=-1)).astype(jnp.int32)
    kept_dev = (place_index < CAP) & to_devices(live_bool)
    route_dev = to_devices(route_ids)
    wide_ids = jnp.arange(N_WIDE, dtype=jnp.int32)[:, None, None]
    narrow_ids = jnp.arange(N_NARROW, dtype=jnp.int32)[None, :, None]
    slot_dev = ((route_dev * N_NARROW + narrow_ids) * N_WIDE + wide_ids) * CAP + place_index
    slot_dev = jnp.where(kept_dev, slot_dev, EXPERTS * N_NARROW * N_WIDE * CAP).astype(jnp.int32)
    slot_index = from_devices(slot_dev)
    kept_mask = from_devices(kept_dev).astype(jnp.float32)
    chosen = chosen_int.astype(jnp.float32)
    float_args = tuple((member.astype(jnp.float32) for member in (hidden_in, norm_gain_attn, query_weight, key_weight, value_weight, out_weight, bias_table, norm_gain_ffn, router_weight, expert_in, expert_out)))

    def objective(*params):
        return forward(*params, lengths, slot_index, kept_mask, chosen)
    output, pullback = jax.vjp(objective, *float_args)
    grads = pullback(cotangent.astype(jnp.float32))
    return (output, grads[0], grads[1], grads[2], grads[3], grads[4], grads[5], grads[6], grads[7], grads[8], grads[9], grads[10])
```

```python
import jax
import jax.numpy as jnp
from jax import lax
from jax.experimental import pallas as pl
from jax.experimental.pallas import tpu as pltpu
from jax.sharding import PartitionSpec as P

epsilon = 1e-06
bucket_edges = (1, 2, 3, 4, 5, 6, 7, 8, 12, 16, 23, 32, 46, 64, 91)
LOG2E = 1.4426950408889634
LN2 = 0.6931471805599453
TILE = 128
VMEM_LIMIT = 56 * 1024 * 1024
NT = (((1,), (1,)), ((), ()))
NN = (((1,), (0,)), ((), ()))
TN = (((0,), (0,)), ((), ()))
BF16 = jnp.bfloat16
F32 = jnp.float32


def dotf(a, b, dims=NN):
    return lax.dot_general(a, b, dims, preferred_element_type=F32)


def rms_factor(values):
    return lax.rsqrt(jnp.mean(values * values, axis=-1, keepdims=True) + epsilon)


def rms_pull(values, factor, gain, grad):
    normal = values * factor
    scaled = grad * gain
    mean = jnp.mean(scaled * normal, axis=-1, keepdims=True)
    return (scaled - normal * mean) * factor, grad * normal


def bucket_of(offsets, bucket_count):
    magnitude = jnp.abs(offsets)
    bucket = jnp.zeros_like(offsets)
    for border in bucket_edges:
        bucket = bucket + (magnitude >= border).astype(jnp.int32)
    return bucket + bucket_count // 2 * (offsets > 0).astype(jnp.int32)


def pieces(x):
    hi = x.astype(BF16)
    rest = x - hi.astype(F32)
    mid = rest.astype(BF16)
    low = (rest - mid.astype(F32)).astype(BF16)
    return hi, mid, low


def bias_tiles(bias_table):
    buckets, heads = bias_table.shape
    place = jnp.arange(TILE, dtype=jnp.int32)
    shift = jnp.arange(-1, 2, dtype=jnp.int32) * TILE
    offsets = shift[:, None, None] + place[None, :, None] - place[None, None, :]
    bucket = bucket_of(offsets, buckets)[None]
    table = bias_table.T * LOG2E
    tiles = jnp.zeros((heads, 3, TILE, TILE), F32)
    for row in range(buckets):
        tiles = jnp.where(bucket == row, table[:, row][:, None, None, None], tiles)
    left = tiles[:, :1] - table[:, buckets // 2 - 1][:, None, None, None]
    right = tiles[:, 2:] - table[:, buckets - 1][:, None, None, None]
    return jnp.concatenate((tiles, left, right), axis=1)


def query_lanes(bias_table, rows):
    buckets, heads = bias_table.shape
    count = rows // TILE
    left = pieces(bias_table[buckets // 2 - 1] * LOG2E)
    right = pieces(bias_table[buckets - 1] * LOG2E)
    one, zero = jnp.ones((heads,), BF16), jnp.zeros((heads,), BF16)
    blocks = []
    for a in range(count):
        lanes = [zero] * 3 + list(left) + list(right)
        for t in range(count):
            lanes += list(left) if t <= a - 2 else list(right) if t >= a + 2 else [zero] * 3
        lanes += [one]
        lanes += [zero] * (64 - len(lanes))
        blocks.append(jnp.stack(lanes + lanes, axis=1))
    pattern = jnp.stack(blocks, axis=1)
    return jnp.broadcast_to(pattern[:, :, None, :], (heads, count, TILE, 128)).reshape(
        heads, rows, 128
    )


def key_lanes(me, lengths, rows):
    count = rows // TILE
    lane = (jnp.arange(128, dtype=jnp.int32) % 64)[None, :]
    place = jnp.arange(rows, dtype=jnp.int32)
    out = []
    for u in range(4):
        block = me ^ u
        base = lane < 3
        base = base | ((lane >= 3) & (lane < 6) & (block < me))
        base = base | ((lane >= 6) & (lane < 9) & (block > me))
        if u == 0:
            for t in range(count):
                own = (place // TILE == t)[:, None]
                base = base | ((lane >= 9 + 3 * t) & (lane < 12 + 3 * t) & own)
        base = jnp.broadcast_to(base, (rows, 128)).astype(F32)
        dead = (block * rows + place)[None, :] >= lengths[:, None]
        masked = (lane == 9 + 3 * count)[None] & dead[:, :, None]
        out.append(jnp.where(masked, -1e30, base[None]).astype(BF16))
    return jnp.stack(out, axis=1)


def neighbour_flags(me):
    one, three = me ^ 1, me ^ 3
    return jnp.stack((one == me + 1, one == me - 1, three == me + 1, three == me - 1)).astype(F32)


def own_lanes(head, rows):
    lane = lax.broadcasted_iota(jnp.int32, (rows, 128), 1)
    return (lane < 64) if head == 0 else (lane >= 64)


def forward_kernel(flags, q, kv, klanes, qlanes, tiles, att, qaug, s_ref):
    rows = q.shape[1]
    count = rows // TILE
    one = jnp.ones((), BF16)
    outs = []
    for h in range(2):
        own = own_lanes(h, rows)
        qa = jnp.where(own, q[0], qlanes[h])
        for u in range(4):
            ka = jnp.where(own, kv[0, u, :, :128], klanes[0, u])
            start = u * rows
            s_ref[h, :, start : start + rows] = dotf(qa, ka, NT)
            if u == 0:
                for a in range(count):
                    for t in range(max(0, a - 1), min(count, a + 2)):
                        spot = (h, slice(a * 128, a * 128 + 128), slice(t * 128, t * 128 + 128))
                        s_ref[spot] = s_ref[spot] + tiles[h, t - a + 1].T
            if u in (1, 3):
                spot = (h, slice(rows - 128, rows), slice(start, start + 128))
                s_ref[spot] = s_ref[spot] + tiles[h, 4].T * flags[u - 1]
                spot = (h, slice(0, 128), slice(start + rows - 128, start + rows))
                s_ref[spot] = s_ref[spot] + tiles[h, 3].T * flags[u]
        top = jnp.max(s_ref[h], axis=1, keepdims=True)
        total = None
        for u in range(4):
            weights = jnp.exp2(s_ref[h, :, u * rows : (u + 1) * rows] - top).astype(BF16)
            part = dotf(weights, jnp.where(own, kv[0, u, :, 128:], one))
            total = part if total is None else total + part
        turned = pltpu.roll(total, 64, 1)
        outs.append(total / turned)
        hi, mid, low = pieces(top + jnp.log2(jnp.where(own, turned, total)))
        lane = lax.broadcasted_iota(jnp.int32, (rows, 128), 1) - (64 if h == 0 else 0)
        qaug[0, h] = jnp.where(
            lane == 0, -hi, jnp.where(lane == 1, -mid, jnp.where(lane == 2, -low, qa))
        )
    att[0] = jnp.where(own_lanes(0, rows), outs[0], outs[1]).astype(BF16)


def attend_forward(flags, q, kv, klanes, qlanes, tiles):
    seqs, rows, width = q.shape
    pairs = width // 128
    heads_block = pl.BlockSpec((1, rows, 128), lambda s, p: (s, 0, p))
    return pl.pallas_call(
        forward_kernel,
        grid=(seqs, pairs),
        in_specs=[
            pl.BlockSpec(memory_space=pltpu.SMEM),
            heads_block,
            pl.BlockSpec((1, 4, rows, 256), lambda s, p: (s, 0, 0, p)),
            pl.BlockSpec((1, 4, rows, 128), lambda s, p: (s, 0, 0, 0)),
            pl.BlockSpec((2, rows, 128), lambda s, p: (p, 0, 0)),
            pl.BlockSpec((2, 5, TILE, TILE), lambda s, p: (p, 0, 0, 0)),
        ],
        out_specs=[heads_block, pl.BlockSpec((1, 2, rows, 128), lambda s, p: (s, p, 0, 0))],
        out_shape=[
            jax.ShapeDtypeStruct((seqs, rows, width), BF16),
            jax.ShapeDtypeStruct((seqs, 2 * pairs, rows, 128), BF16),
        ],
        scratch_shapes=[pltpu.VMEM((2, rows, 4 * rows), F32)],
        compiler_params=pltpu.CompilerParams(
            dimension_semantics=("arbitrary", "arbitrary"), vmem_limit_bytes=VMEM_LIMIT
        ),
        cost_estimate=pl.CostEstimate(
            flops=seqs * 16 * rows * rows * 128 * 2 * pairs,
            bytes_accessed=seqs * rows * width * 24,
            transcendentals=seqs * 8 * pairs * rows * rows,
        ),
        name="attend_forward",
    )(flags, q, kv, klanes, qlanes, tiles)


def backward_kernel(flags, qaug, kv, att, do, klanes, tiles, dq, dkv, table):
    rows = do.shape[1]
    count = rows // TILE
    own0 = own_lanes(0, rows)
    prod = do[0].astype(F32) * att[0].astype(F32)
    one, zero = jnp.ones((), BF16), jnp.zeros((), BF16)
    turned = []
    for h in range(2):
        own = own_lanes(h, rows)
        qa = qaug[0, h]
        delta = jnp.sum(jnp.where(own, prod, 0.0), axis=1, keepdims=True)
        hi, mid, _ = pieces(jnp.broadcast_to(delta, (rows, 128)))
        lane = lax.broadcasted_iota(jnp.int32, (rows, 128), 1) - (64 if h == 0 else 0)
        doa = jnp.where(own, do[0], jnp.where(lane == 0, -hi, jnp.where(lane == 1, -mid, zero)))
        near = {}
        corner = {-1: None, 1: None}
        dqt = None
        for u in range(4):
            ka = jnp.where(own, kv[0, u, :, :128], klanes[0, u])
            va = jnp.where(own, kv[0, u, :, 128:], one)
            st = dotf(ka, qa, NT)
            if u == 0:
                strips = []
                for t in range(count):
                    row = []
                    for a in range(count):
                        x = st[t * 128 : t * 128 + 128, a * 128 : a * 128 + 128]
                        row.append(x + tiles[h, t - a + 1] if abs(t - a) <= 1 else x)
                    strips.append(jnp.concatenate(row, axis=1))
                st = jnp.concatenate(strips, axis=0)
            if u in (1, 3):
                after, before = flags[u - 1], flags[u]
                first = jnp.concatenate(
                    (st[:128, : rows - 128], st[:128, rows - 128 :] + tiles[h, 4] * after), axis=1
                )
                last = jnp.concatenate(
                    (st[rows - 128 :, :128] + tiles[h, 3] * before, st[rows - 128 :, 128:]), axis=1
                )
                st = jnp.concatenate((first, st[128 : rows - 128], last), axis=0)
            probs = jnp.exp2(st)
            ds = probs * dotf(va, doa, NT)
            probs_low, ds_low = probs.astype(BF16), ds.astype(BF16)
            if u == 0:
                for d in (-1, 0, 1):
                    for a in range(max(0, -d), min(count, count - d)):
                        t = a + d
                        x = ds[t * 128 : t * 128 + 128, a * 128 : a * 128 + 128]
                        near[d] = near[d] + x if d in near else x
            if u in (1, 3):
                for d, x in ((1, ds[:128, rows - 128 :] * after), (-1, ds[rows - 128 :, :128] * before)):
                    corner[d] = x if corner[d] is None else corner[d] + x
            dv = dotf(probs_low, doa).astype(BF16)
            dk = (dotf(ds_low, qa) * LN2).astype(BF16)
            if h == 0:
                dkv[0, u, :, :128], dkv[0, u, :, 128:] = dk, dv
            else:
                dkv[0, u, :, :128] = jnp.where(own0, dkv[0, u, :, :128], dk)
                dkv[0, u, :, 128:] = jnp.where(own0, dkv[0, u, :, 128:], dv)
            part = dotf(ka.T, ds_low)
            dqt = part if dqt is None else dqt + part
        turned.append(dqt.T)
        group = lax.broadcasted_iota(jnp.int32, (TILE, TILE), 0) // 8 * 8
        upper = lax.broadcasted_iota(jnp.int32, (TILE, TILE), 1) >= group
        before, after = near[-1] + corner[-1], near[1] + corner[1]
        inner = (jnp.where(upper, near[0], before), jnp.where(upper, after, near[0]))
        for i, x in enumerate(inner):
            lined = x[:8]
            for g in range(1, TILE // 8):
                lined = lined + pltpu.roll(x[8 * g : 8 * g + 8], TILE - 8 * g, 1)
            table[0, h, 8 * i : 8 * i + 8, :] = lined
        outer = (jnp.where(upper, before, 0.0), jnp.where(upper, 0.0, after), corner[-1], corner[1])
        for i, x in enumerate(outer):
            table[0, h, 16 + i : 17 + i, :] = jnp.sum(x, axis=0, keepdims=True)
    dq[0] = (jnp.where(own0, turned[0], turned[1]) * 0.125).astype(BF16)
    for h in range(2):
        for a in range(count):
            rest = jnp.sum(turned[h][a * 128 : a * 128 + 128], axis=0, keepdims=True)
            table[0, h, 20 + a : 21 + a, :] = rest


def attend_backward(flags, qaug, kv, att, do, klanes, tiles):
    seqs, rows, width = do.shape
    pairs = width // 128
    heads_block = pl.BlockSpec((1, rows, 128), lambda s, p: (s, 0, p))
    pair_block = pl.BlockSpec((1, 4, rows, 256), lambda s, p: (s, 0, 0, p))
    return pl.pallas_call(
        backward_kernel,
        grid=(seqs, pairs),
        in_specs=[
            pl.BlockSpec(memory_space=pltpu.SMEM),
            pl.BlockSpec((1, 2, rows, 128), lambda s, p: (s, p, 0, 0)),
            pair_block,
            heads_block,
            heads_block,
            pl.BlockSpec((1, 4, rows, 128), lambda s, p: (s, 0, 0, 0)),
            pl.BlockSpec((2, 5, TILE, TILE), lambda s, p: (p, 0, 0, 0)),
        ],
        out_specs=[
            heads_block,
            pair_block,
            pl.BlockSpec((1, 2, 32, 128), lambda s, p: (s, p, 0, 0)),
        ],
        out_shape=[
            jax.ShapeDtypeStruct((seqs, rows, width), BF16),
            jax.ShapeDtypeStruct((seqs, 4, rows, 2 * width), BF16),
            jax.ShapeDtypeStruct((seqs, 2 * pairs, 32, 128), F32),
        ],
        compiler_params=pltpu.CompilerParams(
            dimension_semantics=("arbitrary", "arbitrary"), vmem_limit_bytes=VMEM_LIMIT
        ),
        cost_estimate=pl.CostEstimate(
            flops=seqs * 40 * rows * rows * 128 * 2 * pairs,
            bytes_accessed=seqs * rows * width * 40,
            transcendentals=seqs * 8 * pairs * rows * rows,
        ),
        name="attend_backward",
    )(flags, qaug, kv, att, do, klanes, tiles)


def table_grad(table, rows, bucket_count):
    count = rows // TILE
    heads = table.shape[0]
    row = jnp.arange(16, dtype=jnp.int32)[:, None]
    lane = jnp.arange(TILE, dtype=jnp.int32)[None, :]
    bucket = bucket_of(row // 8 * TILE + row % 8 - lane, bucket_count)
    ids = jnp.arange(bucket_count, dtype=jnp.int32)
    onehot = (bucket[None] == ids[:, None, None]).astype(F32)
    near = jnp.einsum("hil,bil->bh", table[:, :16], onehot, precision=lax.Precision.HIGHEST)
    halves = table[:, 20 : 20 + count].reshape(heads // 2, 2, count, 2, 64)
    rest = jnp.stack((halves[:, 0, :, 1], halves[:, 1, :, 0]), axis=1).reshape(heads, count, 64)
    outer = jnp.sum(table[:, 16:20], axis=2)
    left = jnp.sum(rest[:, :, 3], axis=1) + outer[:, 0] - outer[:, 2]
    right = jnp.sum(rest[:, :, 6], axis=1) + outer[:, 1] - outer[:, 3]
    for a in range(count):
        for t in range(count):
            if t <= a - 2:
                left = left + rest[:, a, 9 + 3 * t]
            if t >= a + 2:
                right = right + rest[:, a, 9 + 3 * t]
    far = jnp.where((ids == bucket_count // 2 - 1)[:, None], left[None, :], 0.0)
    return near + far + jnp.where((ids == bucket_count - 1)[:, None], right[None, :], 0.0)


def expert_kernel(own, x, c, units, w_in, w_out, router, hidden, grad_pre, low_c, back, grad_x,
                  grad_logits, gate_ref, probs_ref, out_acc, x_acc):
    step = pl.program_id(0)
    rows = x.shape[0]
    chunk = TILE

    @pl.when(step == 0)
    def _():
        logits = dotf(x[...], router[...])
        weights = jnp.exp(logits - jnp.max(logits, axis=1, keepdims=True))
        probs = weights / jnp.sum(weights, axis=1, keepdims=True)
        probs_ref[...] = probs
        ids = lax.broadcasted_iota(jnp.int32, probs.shape, 1)
        gate = jnp.sum(jnp.where(ids == own[0], probs, 0.0), axis=1, keepdims=True)
        gate_ref[...] = jnp.broadcast_to(gate, gate_ref.shape)
        low_c[...] = (c[...].astype(F32) * gate).astype(BF16)
        out_acc[...] = jnp.zeros_like(out_acc)
        x_acc[...] = jnp.zeros_like(x_acc)

    for r in range(rows // chunk):
        part = slice(r * chunk, r * chunk + chunk)
        pre = dotf(x[part, :], w_in[0])
        below = 0.5 + 0.5 * lax.erf(pre * 0.7071067811865476)
        hid = (pre * below).astype(BF16)
        slope = below + pre * (jnp.exp(pre * pre * -0.5) * 0.3989422804014327)
        gate = gate_ref[part, :1]
        low = (slope * gate * units[part, :].astype(F32)).astype(BF16)
        hidden[part, :] = hid
        grad_pre[part, :] = low
        out_acc[part, :] += dotf(hid, w_out[0])
        x_acc[part, :] += dotf(low, w_in[0], NT)

    @pl.when(step == pl.num_programs(0) - 1)
    def _():
        result = out_acc[...]
        gate = gate_ref[:, :1]
        probs = probs_ref[...]
        grad_gate = jnp.sum(c[...].astype(F32) * result.astype(BF16).astype(F32), axis=1, keepdims=True)
        ids = lax.broadcasted_iota(jnp.int32, probs.shape, 1)
        mine = jnp.where(ids == own[0], 1.0, 0.0)
        low = (grad_gate * probs * (mine - gate)).astype(BF16)
        grad_logits[...] = low
        back[...] = (result * gate).astype(BF16)
        grad_x[...] = (x_acc[...] + dotf(low, router[...], NT)).astype(BF16)


def run_expert(own, index, x, c, units, w_in, w_out, router):
    rows, width = x.shape
    hid = w_in.shape[2]
    experts = router.shape[1]
    step = 768
    whole = lambda f: (0, 0)
    sliced = lambda f: (0, f)
    return pl.pallas_call(
        expert_kernel,
        grid=(hid // step,),
        in_specs=[
            pl.BlockSpec(memory_space=pltpu.SMEM),
            pl.BlockSpec((rows, width), whole),
            pl.BlockSpec((rows, width), whole),
            pl.BlockSpec((rows, step), sliced),
            pl.BlockSpec((1, width, step), lambda f: (index, 0, f)),
            pl.BlockSpec((1, step, width), lambda f: (index, f, 0)),
            pl.BlockSpec((width, experts), whole),
        ],
        out_specs=[
            pl.BlockSpec((rows, step), sliced),
            pl.BlockSpec((rows, step), sliced),
            pl.BlockSpec((rows, width), whole),
            pl.BlockSpec((rows, width), whole),
            pl.BlockSpec((rows, width), whole),
            pl.BlockSpec((rows, experts), whole),
        ],
        out_shape=[
            jax.ShapeDtypeStruct((rows, hid), BF16),
            jax.ShapeDtypeStruct((rows, hid), BF16),
            jax.ShapeDtypeStruct((rows, width), BF16),
            jax.ShapeDtypeStruct((rows, width), BF16),
            jax.ShapeDtypeStruct((rows, width), BF16),
            jax.ShapeDtypeStruct((rows, experts), BF16),
        ],
        scratch_shapes=[
            pltpu.VMEM((rows, 128), F32),
            pltpu.VMEM((rows, experts), F32),
            pltpu.VMEM((rows, width), F32),
            pltpu.VMEM((rows, width), F32),
        ],
        compiler_params=pltpu.CompilerParams(
            dimension_semantics=("arbitrary",), vmem_limit_bytes=VMEM_LIMIT
        ),
        cost_estimate=pl.CostEstimate(
            flops=6 * rows * width * hid,
            bytes_accessed=4 * width * hid + 6 * rows * hid,
            transcendentals=2 * rows * hid,
        ),
        name="run_expert",
    )(own, x, c, units, w_in, w_out, router)


def swap(x, bit):
    return lax.ppermute(x, "narrow", [(i, i ^ bit) for i in range(4)])


def gather_blocks(own):
    half = own.shape[0] // 2
    one, two = swap(own, 1), swap(own, 2)
    three = jnp.concatenate((swap(two[:half], 1), swap(one[half:], 2)), axis=0)
    return jnp.stack((own, one, two, three))


def scatter_blocks(blocks):
    half = blocks[0].shape[0] // 2
    low = [b.astype(BF16) for b in blocks]
    from_one = swap(low[3][:half], 1).astype(F32)
    from_two = swap(low[3][half:], 2).astype(F32)
    one = jnp.concatenate((blocks[1][:half], blocks[1][half:] + from_two), axis=0).astype(BF16)
    two = jnp.concatenate((blocks[2][:half] + from_one, blocks[2][half:]), axis=0).astype(BF16)
    return blocks[0] + swap(one, 1).astype(F32) + swap(two, 2).astype(F32)


def after(x, *others):
    return lax.optimization_barrier((x,) + others)[0]


def on_device(
    hidden_in,
    lengths,
    routes,
    norm_gain_attn,
    query_weight,
    key_weight,
    value_weight,
    out_weight,
    bias_table,
    norm_gain_ffn,
    router_weight,
    expert_in,
    expert_out,
    cotangent,
):
    wide_count = lax.axis_size("wide")
    seq_count, rows, width = hidden_in.shape
    bucket_count, head_count = bias_table.shape
    pairs = width // 128
    tokens = seq_count * rows
    local_experts = expert_in.shape[0]
    expert_count = local_experts * wide_count
    capacity = 5 * tokens // (4 * expert_count)
    slots = wide_count * capacity
    me = lax.axis_index("narrow")
    mine = lax.axis_index("wide") * local_experts

    source = hidden_in.astype(F32).reshape(tokens, width)
    factor_attn = rms_factor(source)
    normed = (source * factor_attn * norm_gain_attn).astype(BF16)
    normed_seqs = normed.reshape(seq_count, rows, width)
    pair_weight = jnp.stack(
        (key_weight.reshape(width, pairs, 128), value_weight.reshape(width, pairs, 128)), axis=2
    ).reshape(width, 2 * width)
    blocks = [gather_blocks(normed_seqs[s]) for s in range(seq_count)]
    expert_in, expert_out, _ = lax.optimization_barrier((expert_in, expert_out, blocks[-1]))
    whole_in = lax.all_gather(expert_in, "narrow", axis=2, tiled=True)
    whole_out = lax.all_gather(expert_out, "narrow", axis=1, tiled=True)

    queries = (dotf(normed, query_weight) * (LOG2E / 8)).astype(BF16).reshape(seq_count, rows, width)
    flags = neighbour_flags(me)
    klanes = key_lanes(me, lengths, rows)
    qlanes = query_lanes(bias_table, rows)
    tiles = bias_tiles(bias_table)

    route = routes.reshape(tokens)
    position = me * rows + jnp.arange(rows, dtype=jnp.int32)
    live = (position[None, :] < lengths[:, None]).reshape(tokens)
    expert_ids = jnp.arange(expert_count, dtype=jnp.int32)
    chosen = ((route[:, None] == expert_ids[None, :]) & live[:, None]).astype(F32)
    token_ids = jnp.arange(tokens, dtype=jnp.int32)
    earlier = (token_ids[:, None] > token_ids[None, :]).astype(BF16)
    place = jnp.sum(dotf(earlier, chosen.astype(BF16)) * chosen, axis=-1).astype(jnp.int32)
    kept = live & (place < capacity)
    slot = route // local_experts * capacity + place
    slot_ids = jnp.arange(slots, dtype=jnp.int32)
    maps, cots = [], []
    for e in range(local_experts):
        due = jnp.where(kept & (route % local_experts == e), slot, -1)
        maps.append((slot_ids[:, None] == due[None, :]).astype(BF16))

    def to_experts(values, e):
        sent = dotf(maps[e], values).astype(BF16).reshape(wide_count, capacity, width)
        return lax.all_to_all(sent, "wide", 0, 0, tiled=True).reshape(slots, width)

    def to_tokens(values, e):
        sent = values.reshape(wide_count, capacity, width)
        got = lax.all_to_all(sent, "wide", 0, 0, tiled=True).reshape(slots, width)
        return dotf(maps[e], got, TN)

    cot = cotangent.reshape(tokens, width)
    cots = [to_experts(cot, e) for e in range(local_experts)]

    kvs, atts, qaugs = [], [], []
    for s in range(seq_count):
        kv = dotf(blocks[s].reshape(4 * rows, width), pair_weight).astype(BF16)
        kvs.append(kv.reshape(1, 4, rows, 2 * width))
        att, qaug = attend_forward(flags, queries[s : s + 1], kvs[s], klanes[s : s + 1], qlanes, tiles)
        atts.append(att)
        qaugs.append(qaug)
    attended = jnp.concatenate(atts, axis=0).reshape(tokens, width)
    residual = source + dotf(attended, out_weight)
    factor_ffn = rms_factor(residual)
    ffn_input = (residual * factor_ffn * norm_gain_ffn).astype(BF16)

    xs = [to_experts(ffn_input, e) for e in range(local_experts)]
    units = [dotf(cots[e], whole_out[e], NT).astype(BF16) for e in range(local_experts)]
    results, grad_rows, grad_in, grad_out, grad_router = [], [], [], [], 0.0
    for e in range(local_experts):
        own = jnp.reshape(mine + e, (1,))
        hidden, grad_pre, low_c, back, grad_x, grad_logits = run_expert(
            own, e, xs[e], cots[e], units[e], whole_in, whole_out, router_weight
        )
        grad_rows.append(to_tokens(grad_x, e))
        results.append(back)
        grad_in.append(dotf(xs[e], grad_pre, TN).astype(BF16))
        grad_out.append(dotf(hidden, low_c, TN).astype(BF16))
        grad_router = grad_router + dotf(xs[e], grad_logits, TN)
    grad_expert_in = lax.psum_scatter(
        jnp.stack(grad_in), "narrow", scatter_dimension=2, tiled=True
    ).astype(F32)
    grad_expert_out = lax.psum_scatter(
        jnp.stack(grad_out), "narrow", scatter_dimension=1, tiled=True
    ).astype(F32)

    grad_ffn_input = sum(grad_rows)
    grad_top = cot.astype(F32)
    grad_norm, gain_ffn = rms_pull(residual, factor_ffn, norm_gain_ffn, grad_ffn_input)
    gain_ffn = jnp.sum(gain_ffn, axis=0)
    grad_residual = grad_top + grad_norm
    grad_branch = grad_residual.astype(BF16)
    grad_out_weight = dotf(attended, grad_branch, TN)
    grad_attended = dotf(grad_branch, out_weight, NT).astype(BF16).reshape(seq_count, rows, width)

    results = [to_tokens(after(results[e], grad_branch), e) for e in range(local_experts)]
    block_out = residual + sum(results)

    dqs, dkvs, tables = [], [], []
    for s in range(seq_count):
        dq, dkv, table = attend_backward(
            flags, qaugs[s], kvs[s], atts[s], grad_attended[s : s + 1], klanes[s : s + 1], tiles
        )
        dqs.append(dq)
        dkvs.append(dkv)
        tables.append(table)
    grad_table = table_grad(sum(tables)[0], rows, bucket_count)
    grad_queries = jnp.concatenate(dqs, axis=0).reshape(tokens, width)
    grad_pairs = jnp.concatenate(dkvs, axis=0)
    normed_all = jnp.stack(blocks)
    grad_q = dotf(normed, grad_queries, TN)
    grad_kv = dotf(
        normed_all.reshape(4 * tokens, width), grad_pairs.reshape(4 * tokens, 2 * width), TN
    )
    parts = []
    for s in range(seq_count):
        part = dotf(dkvs[s].reshape(4 * rows, 2 * width), pair_weight, NT).reshape(4, rows, width)
        parts.append(scatter_blocks([part[u] for u in range(4)]))
    grad_normed = jnp.concatenate(parts, axis=0) + dotf(grad_queries, query_weight, NT)
    grad_source, gain_attn = rms_pull(source, factor_attn, norm_gain_attn, grad_normed)
    gain_attn = jnp.sum(gain_attn, axis=0)
    grad_hidden = grad_residual + grad_source

    summed = lax.psum(
        (grad_q, grad_kv, grad_out_weight, grad_router, grad_table, gain_attn, gain_ffn),
        ("narrow", "wide"),
    )
    sum_kv = summed[1].reshape(width, pairs, 2, 128)
    out_shape = (seq_count, rows, width)
    return (
        block_out.reshape(out_shape),
        grad_hidden.reshape(out_shape),
        summed[5],
        summed[0],
        sum_kv[:, :, 0].reshape(width, width),
        sum_kv[:, :, 1].reshape(width, width),
        summed[2],
        summed[4],
        summed[6],
        summed[3],
        grad_expert_in,
        grad_expert_out,
    )


def solution(mesh):
    placed = (
        P("wide", "narrow", None),
        P("wide"),
        P("wide", "narrow", None),
        P(),
        P(),
        P(),
        P(),
        P(),
        P(),
        P(),
        P(),
        P("wide", None, "narrow"),
        P("wide", "narrow", None),
        P("wide", "narrow", None),
    )
    return jax.shard_map(
        on_device,
        mesh=mesh,
        in_specs=placed,
        out_specs=(
            P("wide", "narrow", None),
            P("wide", "narrow", None),
            P(),
            P(),
            P(),
            P(),
            P(),
            P(),
            P(),
            P(),
            P("wide", None, "narrow"),
            P("wide", "narrow", None),
        ),
        check_vma=False,
    )
```

```python
import functools

import jax
import jax.numpy as jnp
import numpy as np
from jax import lax
from jax.experimental import pallas as pl
from jax.experimental.pallas import tpu as pltpu
from jax.sharding import PartitionSpec as P

epsilon = 1e-06
bucket_edges = (1, 2, 3, 4, 5, 6, 7, 8, 12, 16, 23, 32, 46, 64, 91)
LOG2E = 1.4426950408889634
LN2 = 0.6931471805599453
TILE = 128
VMEM_LIMIT = 56 * 1024 * 1024
NT = (((1,), (1,)), ((), ()))
NN = (((1,), (0,)), ((), ()))
TN = (((0,), (0,)), ((), ()))
BRIEF = pl.CostEstimate(flops=1, bytes_accessed=1, transcendentals=0)
LONG = pl.CostEstimate(flops=12_000_000_000, bytes_accessed=1, transcendentals=0)
BF16 = jnp.bfloat16
F32 = jnp.float32


def dotf(a, b, dims=NN):
    return lax.dot_general(a, b, dims, preferred_element_type=F32)


def rms_factor(values):
    return lax.rsqrt(jnp.mean(values * values, axis=-1, keepdims=True) + epsilon)


def rms_pull(values, factor, gain, grad):
    normal = values * factor
    scaled = grad * gain
    mean = jnp.mean(scaled * normal, axis=-1, keepdims=True)
    return (scaled - normal * mean) * factor, grad * normal


def bucket_of(offsets, bucket_count):
    magnitude = jnp.abs(offsets)
    bucket = jnp.zeros_like(offsets)
    for border in bucket_edges:
        bucket = bucket + (magnitude >= border).astype(jnp.int32)
    return bucket + bucket_count // 2 * (offsets > 0).astype(jnp.int32)


def pieces(x):
    hi = x.astype(BF16)
    rest = x - hi.astype(F32)
    mid = rest.astype(BF16)
    low = (rest - mid.astype(F32)).astype(BF16)
    return hi, mid, low


def tiles_kernel(rows, tiles):
    heads = tiles.shape[0]
    for h in range(heads):
        for d in range(3):
            values = jnp.broadcast_to(rows[h : h + 1, d * TILE : d * TILE + 2 * TILE], (TILE, 2 * TILE))
            moved = pltpu.roll(values, 0, 1, stride=1, stride_axis=0)[:, TILE:].T
            tiles[h, d] = moved
            if d == 0:
                tiles[h, 3] = moved - rows[h : h + 1, 4 * TILE : 5 * TILE]
            if d == 2:
                tiles[h, 4] = moved - rows[h : h + 1, 5 * TILE :]


def bias_tiles(bias_table):
    buckets, heads = bias_table.shape
    bucket = bucket_of(jnp.arange(4 * TILE, dtype=jnp.int32) - 2 * TILE, buckets)
    ends = jnp.repeat(jnp.array([buckets // 2 - 1, buckets - 1], jnp.int32), TILE)
    onehot = jnp.concatenate((bucket, ends))[None] == jnp.arange(buckets, dtype=jnp.int32)[:, None]
    rows = lax.dot_general(
        bias_table * LOG2E, onehot.astype(F32), TN, precision=lax.Precision.HIGHEST
    )
    return pl.pallas_call(
        tiles_kernel,
        out_shape=jax.ShapeDtypeStruct((heads, 5, TILE, TILE), F32),
        name="bias_tiles",
    )(rows)


def query_lanes(bias_table, rows):
    buckets, heads = bias_table.shape
    count = rows // TILE
    code = np.zeros((count, 128), np.int32)
    for lane in range(128):
        k = lane % 64
        for a in range(count):
            if 3 <= k < 9:
                code[a, lane] = k - 2
            elif 9 <= k < 9 + 3 * count:
                t = (k - 9) // 3
                code[a, lane] = 1 + k % 3 if t <= a - 2 else 4 + k % 3 if t >= a + 2 else 0
            elif k == 9 + 3 * count:
                code[a, lane] = 7
    values = pieces(bias_table[buckets // 2 - 1] * LOG2E) + pieces(bias_table[buckets - 1] * LOG2E)
    values = values + (jnp.ones((heads,), BF16),)
    code = jnp.asarray(np.repeat(code, TILE, axis=0))[None]
    lanes = jnp.zeros((heads, rows, 128), BF16)
    for i, value in enumerate(values):
        lanes = jnp.where(code == i + 1, value[:, None, None], lanes)
    return lanes


def key_lanes(me, lengths, rows):
    count = rows // TILE
    shape = (lengths.shape[0], 4, rows, 128)
    lane = lax.broadcasted_iota(jnp.int32, shape, 3) % 64
    place = lax.broadcasted_iota(jnp.int32, shape, 2)
    u = lax.broadcasted_iota(jnp.int32, shape, 1)
    block = me ^ u
    one = lane < 3
    one = one | ((lane >= 3) & (lane < 6) & (block < me))
    one = one | ((lane >= 6) & (lane < 9) & (block > me))
    one = one | ((u == 0) & (lane >= 9) & (lane < 9 + 3 * count) & ((lane - 9) // 3 == place // TILE))
    dead = block * rows + place >= lengths[:, None, None, None]
    masked = (lane == 9 + 3 * count) & dead
    return jnp.where(masked, -1e30, one.astype(F32)).astype(BF16)


def neighbour_flags(me):
    one, three = me ^ 1, me ^ 3
    return jnp.stack((one == me + 1, one == me - 1, three == me + 1, three == me - 1)).astype(F32)


def own_lanes(head, rows):
    lane = lax.broadcasted_iota(jnp.int32, (rows, 128), 1)
    return (lane < 64) if head == 0 else (lane >= 64)


def forward_kernel(flags, q, keys, values, klanes, qlanes, tiles, att, qaug, s_ref):
    rows = q.shape[1]
    count = rows // TILE
    one = jnp.ones((), BF16)
    outs = []
    for h in range(2):
        own = own_lanes(h, rows)
        qa = jnp.where(own, q[0], qlanes[h])
        for u in range(4):
            ka = jnp.where(own, keys[0, u], klanes[0, u])
            start = u * rows
            s_ref[h, :, start : start + rows] = dotf(qa, ka, NT)
            if u == 0:
                for a in range(count):
                    for t in range(max(0, a - 1), min(count, a + 2)):
                        spot = (h, slice(a * 128, a * 128 + 128), slice(t * 128, t * 128 + 128))
                        s_ref[spot] = s_ref[spot] + tiles[h, t - a + 1].T
            if u in (1, 3):
                spot = (h, slice(rows - 128, rows), slice(start, start + 128))
                s_ref[spot] = s_ref[spot] + tiles[h, 4].T * flags[u - 1]
                spot = (h, slice(0, 128), slice(start + rows - 128, start + rows))
                s_ref[spot] = s_ref[spot] + tiles[h, 3].T * flags[u]
        top = jnp.max(s_ref[h], axis=1, keepdims=True)
        total = None
        for u in range(4):
            weights = jnp.exp2(s_ref[h, :, u * rows : (u + 1) * rows] - top).astype(BF16)
            part = dotf(weights, jnp.where(own, values[0, u], one))
            total = part if total is None else total + part
        turned = pltpu.roll(total, 64, 1)
        outs.append(total / turned)
        hi, mid, low = pieces(top + jnp.log2(jnp.where(own, turned, total)))
        lane = lax.broadcasted_iota(jnp.int32, (rows, 128), 1) - (64 if h == 0 else 0)
        qaug[0, h] = jnp.where(
            lane == 0, -hi, jnp.where(lane == 1, -mid, jnp.where(lane == 2, -low, qa))
        )
    att[0] = jnp.where(own_lanes(0, rows), outs[0], outs[1]).astype(BF16)


def attend_forward(seq, cost, flags, q, keys, values, klanes, qlanes, tiles):
    rows, width = q.shape[1:]
    pairs = width // 128
    return pl.pallas_call(
        forward_kernel,
        grid=(pairs,),
        in_specs=[
            pl.BlockSpec(memory_space=pltpu.SMEM),
            pl.BlockSpec((1, rows, 128), lambda p: (seq, 0, p)),
            pl.BlockSpec((1, 4, rows, 128), lambda p: (0, 0, 0, p)),
            pl.BlockSpec((1, 4, rows, 128), lambda p: (0, 0, 0, p)),
            pl.BlockSpec((1, 4, rows, 128), lambda p: (seq, 0, 0, 0)),
            pl.BlockSpec((2, rows, 128), lambda p: (p, 0, 0)),
            pl.BlockSpec((2, 5, TILE, TILE), lambda p: (p, 0, 0, 0)),
        ],
        out_specs=[
            pl.BlockSpec((1, rows, 128), lambda p: (0, 0, p)),
            pl.BlockSpec((1, 2, rows, 128), lambda p: (0, p, 0, 0)),
        ],
        out_shape=[
            jax.ShapeDtypeStruct((1, rows, width), BF16),
            jax.ShapeDtypeStruct((1, 2 * pairs, rows, 128), BF16),
        ],
        scratch_shapes=[pltpu.VMEM((2, rows, 4 * rows), F32)],
        compiler_params=pltpu.CompilerParams(
            dimension_semantics=("arbitrary",), vmem_limit_bytes=VMEM_LIMIT
        ),
        cost_estimate=cost,
        name="attend_forward",
    )(flags, q, keys, values, klanes, qlanes, tiles)


def backward_kernel(flags, qaug, keys, values, att, do, klanes, tiles, dq, dkeys, dvalues, table):
    rows = do.shape[1]
    count = rows // TILE
    own0 = own_lanes(0, rows)
    prod = do[0].astype(F32) * att[0].astype(F32)
    one, zero = jnp.ones((), BF16), jnp.zeros((), BF16)
    turned = []
    for h in range(2):
        own = own_lanes(h, rows)
        qa = qaug[0, h]
        delta = jnp.sum(jnp.where(own, prod, 0.0), axis=1, keepdims=True)
        hi, mid, _ = pieces(jnp.broadcast_to(delta, (rows, 128)))
        lane = lax.broadcasted_iota(jnp.int32, (rows, 128), 1) - (64 if h == 0 else 0)
        doa = jnp.where(own, do[0], jnp.where(lane == 0, -hi, jnp.where(lane == 1, -mid, zero)))
        near = {}
        corner = {-1: None, 1: None}
        dqt = None
        for u in range(4):
            ka = jnp.where(own, keys[0, u], klanes[0, u])
            va = jnp.where(own, values[0, u], one)
            st = dotf(ka, qa, NT)
            if u == 0:
                strips = []
                for t in range(count):
                    row = []
                    for a in range(count):
                        x = st[t * 128 : t * 128 + 128, a * 128 : a * 128 + 128]
                        row.append(x + tiles[h, t - a + 1] if abs(t - a) <= 1 else x)
                    strips.append(jnp.concatenate(row, axis=1))
                st = jnp.concatenate(strips, axis=0)
            if u in (1, 3):
                after, before = flags[u - 1], flags[u]
                first = jnp.concatenate(
                    (st[:128, : rows - 128], st[:128, rows - 128 :] + tiles[h, 4] * after), axis=1
                )
                last = jnp.concatenate(
                    (st[rows - 128 :, :128] + tiles[h, 3] * before, st[rows - 128 :, 128:]), axis=1
                )
                st = jnp.concatenate((first, st[128 : rows - 128], last), axis=0)
            probs = jnp.exp2(st)
            ds = probs * dotf(va, doa, NT)
            probs_low, ds_low = probs.astype(BF16), ds.astype(BF16)
            if u == 0:
                for d in (-1, 0, 1):
                    for a in range(max(0, -d), min(count, count - d)):
                        t = a + d
                        x = ds[t * 128 : t * 128 + 128, a * 128 : a * 128 + 128]
                        near[d] = near[d] + x if d in near else x
            if u in (1, 3):
                for d, x in ((1, ds[:128, rows - 128 :] * after), (-1, ds[rows - 128 :, :128] * before)):
                    corner[d] = x if corner[d] is None else corner[d] + x
            dv = dotf(probs_low, doa).astype(BF16)
            dk = (dotf(ds_low, qa) * LN2).astype(BF16)
            if h == 0:
                dkeys[0, u], dvalues[0, u] = dk, dv
            else:
                dkeys[0, u] = jnp.where(own0, dkeys[0, u], dk)
                dvalues[0, u] = jnp.where(own0, dvalues[0, u], dv)
            part = dotf(ka.T, ds_low)
            dqt = part if dqt is None else dqt + part
        turned.append(dqt.T)
        group = lax.broadcasted_iota(jnp.int32, (TILE, TILE), 0) // 8 * 8
        upper = lax.broadcasted_iota(jnp.int32, (TILE, TILE), 1) >= group
        before, after = near[-1] + corner[-1], near[1] + corner[1]
        inner = (jnp.where(upper, near[0], before), jnp.where(upper, after, near[0]))
        for i, x in enumerate(inner):
            lined = x[:8]
            for g in range(1, TILE // 8):
                lined = lined + pltpu.roll(x[8 * g : 8 * g + 8], TILE - 8 * g, 1)
            table[0, h, 8 * i : 8 * i + 8, :] = lined
        outer = (jnp.where(upper, before, 0.0), jnp.where(upper, 0.0, after), corner[-1], corner[1])
        for i, x in enumerate(outer):
            table[0, h, 16 + i : 17 + i, :] = jnp.sum(x, axis=0, keepdims=True)
    dq[0] = (jnp.where(own0, turned[0], turned[1]) * 0.125).astype(BF16)
    for h in range(2):
        for a in range(count):
            rest = jnp.sum(turned[h][a * 128 : a * 128 + 128], axis=0, keepdims=True)
            table[0, h, 20 + a : 21 + a, :] = rest


def attend_backward(seq, flags, qaug, keys, values, att, do, klanes, tiles):
    rows, width = do.shape[1:]
    pairs = width // 128
    return pl.pallas_call(
        backward_kernel,
        grid=(pairs,),
        in_specs=[
            pl.BlockSpec(memory_space=pltpu.SMEM),
            pl.BlockSpec((1, 2, rows, 128), lambda p: (0, p, 0, 0)),
            pl.BlockSpec((1, 4, rows, 128), lambda p: (0, 0, 0, p)),
            pl.BlockSpec((1, 4, rows, 128), lambda p: (0, 0, 0, p)),
            pl.BlockSpec((1, rows, 128), lambda p: (0, 0, p)),
            pl.BlockSpec((1, rows, 128), lambda p: (seq, 0, p)),
            pl.BlockSpec((1, 4, rows, 128), lambda p: (seq, 0, 0, 0)),
            pl.BlockSpec((2, 5, TILE, TILE), lambda p: (p, 0, 0, 0)),
        ],
        out_specs=[
            pl.BlockSpec((1, rows, 128), lambda p: (0, 0, p)),
            pl.BlockSpec((1, 4, rows, 128), lambda p: (0, 0, 0, p)),
            pl.BlockSpec((1, 4, rows, 128), lambda p: (0, 0, 0, p)),
            pl.BlockSpec((1, 2, 32, 128), lambda p: (0, p, 0, 0)),
        ],
        out_shape=[
            jax.ShapeDtypeStruct((1, rows, width), BF16),
            jax.ShapeDtypeStruct((1, 4, rows, width), BF16),
            jax.ShapeDtypeStruct((1, 4, rows, width), BF16),
            jax.ShapeDtypeStruct((1, 2 * pairs, 32, 128), F32),
        ],
        compiler_params=pltpu.CompilerParams(
            dimension_semantics=("arbitrary",), vmem_limit_bytes=VMEM_LIMIT
        ),
        cost_estimate=BRIEF,
        name="attend_backward",
    )(flags, qaug, keys, values, att, do, klanes, tiles)


def table_grad(table, rows, bucket_count):
    count = rows // TILE
    heads = table.shape[0]
    row = jnp.arange(16, dtype=jnp.int32)[:, None]
    lane = jnp.arange(TILE, dtype=jnp.int32)[None, :]
    bucket = bucket_of(row // 8 * TILE + row % 8 - lane, bucket_count)
    ids = jnp.arange(bucket_count, dtype=jnp.int32)
    onehot = (bucket[None] == ids[:, None, None]).astype(F32)
    near = jnp.einsum("hil,bil->bh", table[:, :16], onehot, precision=lax.Precision.HIGHEST)
    halves = table[:, 20 : 20 + count].reshape(heads // 2, 2, count, 2, 64)
    rest = jnp.stack((halves[:, 0, :, 1], halves[:, 1, :, 0]), axis=1).reshape(heads, count, 64)
    outer = jnp.sum(table[:, 16:20], axis=2)
    left = jnp.sum(rest[:, :, 3], axis=1) + outer[:, 0] - outer[:, 2]
    right = jnp.sum(rest[:, :, 6], axis=1) + outer[:, 1] - outer[:, 3]
    for a in range(count):
        for t in range(count):
            if t <= a - 2:
                left = left + rest[:, a, 9 + 3 * t]
            if t >= a + 2:
                right = right + rest[:, a, 9 + 3 * t]
    far = jnp.where((ids == bucket_count // 2 - 1)[:, None], left[None, :], 0.0)
    return near + far + jnp.where((ids == bucket_count - 1)[:, None], right[None, :], 0.0)


def expert_kernel(experts, fresh, own, x, c, in0, in1, in2, in3, out0, out1, out2, out3, router, *refs):
    (hidden, grad_pre, low_c, back, grad_x, grad_logits) = refs[0 if fresh else 3 :][:6]
    gate_ref, probs_ref, out_acc, x_acc, w_in, w_out, sems = refs[-7:]
    step = pl.program_id(0)
    ins, outs = (in0, in1, in2, in3), (out0, out1, out2, out3)
    rows = x.shape[0]

    def fetch(u):
        return (
            pltpu.make_async_copy(ins[u], w_in.at[u], sems.at[0, u]),
            pltpu.make_async_copy(outs[u], w_out.at[u], sems.at[1, u]),
        )

    for u in range(4):

        @pl.when(step == max(u - 1, 0))
        def _():
            for copy in fetch(u):
                copy.start()

    @pl.when(step == 0)
    def _():
        ids = lax.broadcasted_iota(jnp.int32, probs_ref.shape, 1)
        logits = jnp.where(ids < experts, dotf(x[...], router[...]), -1e30)
        weights = jnp.exp(logits - jnp.max(logits, axis=1, keepdims=True))
        probs = weights / jnp.sum(weights, axis=1, keepdims=True)
        probs_ref[...] = probs
        gate = jnp.sum(jnp.where(ids == own[0], probs, 0.0), axis=1, keepdims=True)
        gate_ref[...] = jnp.broadcast_to(gate, gate_ref.shape)
        low_c[...] = (c[...].astype(F32) * gate).astype(BF16)
        out_acc[...] = jnp.zeros_like(out_acc)
        x_acc[...] = jnp.zeros_like(x_acc)

    for u in range(4):

        @pl.when(step == u)
        def _():
            for copy in fetch(u):
                copy.wait()

    first, second = w_in[step], w_out[step]
    pre = dotf(x[...], first)
    units = dotf(low_c[...], second, NT)
    below = 0.5 + 0.5 * lax.erf(pre * 0.7071067811865476)
    hid = (pre * below).astype(BF16)
    slope = below + pre * (jnp.exp(pre * pre * -0.5) * 0.3989422804014327)
    low = (slope * units).astype(BF16)
    hidden[0] = hid
    grad_pre[0] = low
    out_acc[...] += dotf(hid, second)
    x_acc[...] += dotf(low, first, NT)

    @pl.when(step == 3)
    def _():
        result = out_acc[...]
        gate = gate_ref[:, :1]
        probs = probs_ref[...]
        grad_gate = jnp.sum(c[...].astype(F32) * result.astype(BF16).astype(F32), axis=1, keepdims=True)
        ids = lax.broadcasted_iota(jnp.int32, probs.shape, 1)
        mine = jnp.where(ids == own[0], 1.0, 0.0)
        logits = (grad_gate * probs * (mine - gate)).astype(BF16)
        grad_logits[...] = logits
        back[...] = (result * gate).astype(BF16)
        grad_x[...] = (x_acc[...] + dotf(logits, router[...], NT)).astype(BF16)


def run_expert(half, experts, own, x, c, ins, outs, router, kept=()):
    rows, width = x.shape
    lanes = router.shape[1]
    whole = lambda u: (0, 0)
    anywhere = pl.BlockSpec(memory_space=pl.ANY)
    blocks = pl.BlockSpec((1, rows, width), lambda u: (u, half, 0))
    both = jax.ShapeDtypeStruct((4, 2 * rows, width), BF16)
    one = jax.ShapeDtypeStruct((rows, width), BF16)
    return pl.pallas_call(
        functools.partial(expert_kernel, experts, not kept),
        grid=(4,),
        in_specs=[
            pl.BlockSpec(memory_space=pltpu.SMEM),
            pl.BlockSpec((rows, width), whole),
            pl.BlockSpec((rows, width), whole),
        ]
        + [anywhere] * 8
        + [pl.BlockSpec((width, lanes), whole)]
        + [anywhere] * len(kept),
        out_specs=[blocks, blocks, pl.BlockSpec((rows, width), lambda u: (half, 0))]
        + [pl.BlockSpec((rows, width), whole)] * 2
        + [pl.BlockSpec((rows, lanes), whole)],
        out_shape=[both, both, jax.ShapeDtypeStruct((2 * rows, width), BF16), one, one]
        + [jax.ShapeDtypeStruct((rows, lanes), BF16)],
        scratch_shapes=[
            pltpu.VMEM((rows, 128), F32),
            pltpu.VMEM((rows, lanes), F32),
            pltpu.VMEM((rows, width), F32),
            pltpu.VMEM((rows, width), F32),
            pltpu.VMEM((4,) + ins[0].shape, BF16),
            pltpu.VMEM((4,) + outs[0].shape, BF16),
            pltpu.SemaphoreType.DMA((2, 4)),
        ],
        input_output_aliases={12 + i: i for i in range(len(kept))},
        compiler_params=pltpu.CompilerParams(
            dimension_semantics=("arbitrary",), vmem_limit_bytes=VMEM_LIMIT
        ),
        cost_estimate=BRIEF,
        name="run_expert",
    )(own, x, c, *ins, *outs, router, *kept)


def swap(x, bit):
    return lax.ppermute(x, "narrow", [(i, i ^ bit) for i in range(4)])


def swap_wide(x, bit):
    return lax.ppermute(x, "wide", [(i, i ^ bit) for i in range(lax.axis_size("wide"))])


def after(x, *others):
    return lax.optimization_barrier((x,) + others)[0]


def pick(x, index):
    return lax.dynamic_index_in_dim(x, index, 0, keepdims=False)


def scatter_blocks(blocks):
    half = blocks[0].shape[0] // 2
    from_one = swap(blocks[3][:half], 1).astype(F32)
    from_two = swap(blocks[3][half:], 2).astype(F32)
    one = jnp.concatenate(
        (blocks[1][:half], (blocks[1][half:].astype(F32) + from_two).astype(BF16)), axis=0
    )
    two = jnp.concatenate(
        ((blocks[2][:half].astype(F32) + from_one).astype(BF16), blocks[2][half:]), axis=0
    )
    return blocks[0].astype(F32) + swap(one, 1).astype(F32) + swap(two, 2).astype(F32)


def sum_everywhere(x):
    wide = lax.axis_index("wide")
    narrow = lax.axis_index("narrow")
    layers = lax.axis_size("wide") // 2
    rows = x.shape[0]
    x = jnp.pad(x.astype(BF16), ((0, -rows % (8 * layers)), (0, 0)))

    def layer_swap(a, k):
        return swap_wide(a, 2 * k)

    levels = ((2, wide % 2, swap_wide), (4, narrow, swap), (layers, wide // 2, layer_swap))
    for count, place, send in levels:
        x = x.reshape(count, x.shape[0] // count, -1)
        total = pick(x, place).astype(F32)
        for k in range(1, count):
            total = total + send(pick(x, place ^ k), k).astype(F32)
        x = total.astype(BF16)
    for count, place, send in reversed(levels):
        parts = jnp.stack([x] + [send(x, k) for k in range(1, count)])
        x = jnp.concatenate([pick(parts, place ^ i) for i in range(count)], axis=0)
    return x[:rows]


def on_device(
    hidden_in,
    lengths,
    routes,
    norm_gain_attn,
    query_weight,
    key_weight,
    value_weight,
    out_weight,
    bias_table,
    norm_gain_ffn,
    router_weight,
    expert_in,
    expert_out,
    cotangent,
):
    wide_count = lax.axis_size("wide")
    seq_count, rows, width = hidden_in.shape
    bucket_count, head_count = bias_table.shape
    pairs = width // 128
    tokens = seq_count * rows
    local_experts = expert_in.shape[0]
    expert_count = local_experts * wide_count
    capacity = 5 * tokens // (4 * expert_count)
    slots = wide_count * capacity
    me = lax.axis_index("narrow")
    near = me // 2
    far = 1 - near
    own = jnp.reshape(lax.axis_index("wide") * local_experts + near, (1,))

    source = hidden_in.astype(F32).reshape(tokens, width)
    factor_attn = rms_factor(source)
    normed = (source * factor_attn * norm_gain_attn).astype(BF16)
    normed_seqs = normed.reshape(seq_count, rows, width)
    queries = (dotf(normed, query_weight) * (LOG2E / 8)).astype(BF16).reshape(seq_count, rows, width)
    flags = neighbour_flags(me)
    klanes = key_lanes(me, lengths, rows)
    qlanes = query_lanes(bias_table, rows)
    tiles = bias_tiles(bias_table)
    router = jnp.pad(router_weight, ((0, 0), (0, -expert_count % 128)))
    shards = [(pick(w, near), pick(w, far)) for w in (expert_in, expert_out)]

    blocks = []
    for s in range(seq_count):
        mine = after(normed_seqs[s], blocks[-1]) if blocks else normed_seqs[s]
        others = [swap(mine, u) for u in range(1, 4)]
        if s == 0:
            first = (others, queries, klanes, qlanes, tiles, router, shards)
            first = lax.optimization_barrier(first)
            others, queries, klanes, qlanes, tiles, router, shards = first
        blocks.append(jnp.stack([mine] + others))

    route = routes.reshape(tokens)
    position = me * rows + jnp.arange(rows, dtype=jnp.int32)
    live = (position[None, :] < lengths[:, None]).reshape(tokens)
    expert_ids = jnp.arange(expert_count, dtype=jnp.int32)
    chosen = ((route[:, None] == expert_ids[None, :]) & live[:, None]).astype(F32)
    token_ids = jnp.arange(tokens, dtype=jnp.int32)
    earlier = (token_ids[:, None] > token_ids[None, :]).astype(BF16)
    place = jnp.sum(dotf(earlier, chosen.astype(BF16)) * chosen, axis=-1).astype(jnp.int32)
    kept = live & (place < capacity)
    slot = route // local_experts * capacity + place
    slot_ids = jnp.arange(slots, dtype=jnp.int32)

    def slot_map(expert):
        due = jnp.where(kept & (route % local_experts == expert), slot, -1)
        return (slot_ids[:, None] == due[None, :]).astype(BF16)

    map_far, map_near = slot_map(far), slot_map(near)

    def exchange(values):
        sent = values.reshape(wide_count, -1, width)
        return lax.all_to_all(sent, "wide", 0, 0, tiled=True)

    cot = cotangent.reshape(tokens, width)
    cot_far = dotf(map_far, cot).astype(BF16).reshape(wide_count, capacity, width)
    cot_near = dotf(map_near, cot).astype(BF16).reshape(wide_count, capacity, width)
    got = exchange(jnp.concatenate((cot_far, cot_near), axis=1).reshape(2 * slots, width))
    cot_far = swap(got[:, :capacity].reshape(slots, width), 2)
    cot_near = got[:, capacity:].reshape(slots, width)

    kvs, atts, qaugs = [], [], []
    for s in range(seq_count):
        rows_all = blocks[s].reshape(4 * rows, width)
        kvs.append(
            [
                dotf(rows_all, w).astype(BF16).reshape(1, 4, rows, width)
                for w in (key_weight, value_weight)
            ]
        )
        cost = LONG if s == 0 else BRIEF
        att, qaug = attend_forward(s, cost, flags, queries, *kvs[s], klanes, qlanes, tiles)
        atts.append(att)
        qaugs.append(qaug)
        if s == 0:
            shards, _ = lax.optimization_barrier((shards, att))
            ins, outs = ([zero, swap(zero, 1), swap(other, 2)] for zero, other in shards)
    attended = jnp.concatenate(atts, axis=0).reshape(tokens, width)
    attended, ins, outs = lax.optimization_barrier((attended, ins, outs))
    residual = source + dotf(attended, out_weight)
    factor_ffn = rms_factor(residual)
    ffn_input = (residual * factor_ffn * norm_gain_ffn).astype(BF16)

    sent_far = dotf(map_far, ffn_input).astype(BF16)
    sent_near = dotf(map_near, after(ffn_input, sent_far, cot_far)).astype(BF16)
    ins.append(swap(after(ins[2], sent_near), 1))
    outs.append(swap(after(outs[2], ins[3]), 1))
    x_far = swap(exchange(sent_far).reshape(slots, width), 2)
    x_near = exchange(sent_near).reshape(slots, width)
    *shared, back_far, grad_x_far, logits_far = run_expert(
        0, expert_count, own, x_far, cot_far, ins, outs, router
    )
    grad_x_far = swap(grad_x_far, 2)
    hidden, grad_pre, low_c, back_near, grad_x_near, logits_near = run_expert(
        1, expert_count, own, x_near, cot_near, ins, outs, router, tuple(shared)
    )
    sent = jnp.concatenate(
        [x.reshape(wide_count, capacity, width) for x in (grad_x_far, grad_x_near)], axis=1
    )
    got = exchange(sent)
    grad_x_far, grad_x_near = (
        x.reshape(slots, width) for x in (got[:, :capacity], got[:, capacity:])
    )

    x_far, x_near, low_c, logits_far, logits_near, _ = lax.optimization_barrier(
        (x_far, x_near, low_c, logits_far, logits_near, sent)
    )
    xs = jnp.concatenate((x_far, x_near), axis=0)
    grad_experts = [None] * 4
    for u in (3, 1, 2, 0):
        both = (dotf(xs, grad_pre[u], TN), dotf(hidden[u], low_c, TN))
        both = jnp.concatenate([x.astype(BF16) for x in both], axis=0)
        grad_experts[u] = swap(both, u) if u else both
    back_far = swap(after(back_far, sent), 2)

    grad_router = dotf(x_far, logits_far, TN) + dotf(x_near, logits_near, TN)

    grad_ffn_input = dotf(map_near, grad_x_near, TN) + dotf(map_far, grad_x_far, TN)
    grad_norm, gain_ffn = rms_pull(residual, factor_ffn, norm_gain_ffn, grad_ffn_input)
    gain_ffn = jnp.sum(gain_ffn, axis=0)
    grad_residual = cot.astype(F32) + grad_norm
    grad_branch = grad_residual.astype(BF16)
    grad_out_weight = dotf(attended, grad_branch, TN)
    grad_attended = dotf(grad_branch, out_weight, NT).astype(BF16).reshape(seq_count, rows, width)
    back = jnp.concatenate(
        [x.reshape(wide_count, capacity, width) for x in (back_far, back_near)], axis=1
    )
    grad_attended, back = lax.optimization_barrier((grad_attended, back))
    back = exchange(back)
    dqs, dks, dvs = [], [], []
    table = 0.0
    for s in range(seq_count):
        dq, dk, dv, table_one = attend_backward(
            s, flags, qaugs[s], *kvs[s], atts[s], after(grad_attended, *dqs), klanes, tiles
        )
        dqs.append(dq.reshape(rows, width))
        dks.append(dk.reshape(4 * rows, width))
        dvs.append(dv.reshape(4 * rows, width))
        table = table + table_one[0]
    dqs, dks, dvs, grad_experts, back = lax.optimization_barrier(
        (dqs, dks, dvs, grad_experts, back)
    )
    summands = [
        sum(dotf(x.reshape(-1, width), g, TN) for x, g in zip(xs, grads))
        for xs, grads in ((normed_seqs, dqs), (blocks, dks), (blocks, dvs))
    ]
    table = table_grad(table, rows, bucket_count)
    rest = jnp.concatenate(
        (
            jnp.pad(table, ((0, 0), (0, width - head_count))),
            grad_router.T[:expert_count],
            gain_ffn[None],
            jnp.zeros((-(bucket_count + expert_count + 1) % 64, width), F32),
        ),
        axis=0,
    )
    summands = [x.astype(BF16) for x in summands + [grad_out_weight, rest]]
    summands, dqs, dks, dvs = lax.optimization_barrier((summands, dqs, dks, dvs))
    sums = sum_everywhere(jnp.concatenate(summands, axis=0)).astype(F32)
    block_out = residual + dotf(map_far, back[:, :capacity].reshape(slots, width), TN)
    block_out = block_out + dotf(map_near, back[:, capacity:].reshape(slots, width), TN)
    zero, one, two, three = (x.astype(F32).reshape(2, 1, width, -1) for x in grad_experts)
    zero, other = zero + one, two + three
    grad_in, grad_out = jnp.where(
        near == 0, jnp.concatenate((zero, other), axis=1), jnp.concatenate((other, zero), axis=1)
    )

    parts = []
    for s in range(seq_count):
        part = dotf(dks[s], key_weight, NT) + dotf(dvs[s], value_weight, NT)
        part = part.astype(BF16).reshape(4, rows, width)
        own_part = dotf(dqs[s], query_weight, NT)
        parts.append(scatter_blocks([part[u] for u in range(4)]) + own_part)
    grad_normed = jnp.concatenate(parts, axis=0)
    grad_hidden = grad_residual + rms_pull(source, factor_attn, norm_gain_attn, grad_normed)[0]

    sum_q, sum_k, sum_v, sum_out = (sums[i * width : (i + 1) * width] for i in range(4))
    sum_rest = sums[4 * width :]
    sum_router = sum_rest[bucket_count : bucket_count + expert_count]
    gain_attn = sum(
        jnp.sum(grad * weight.astype(F32), axis=1)
        for grad, weight in ((sum_q, query_weight), (sum_k, key_weight), (sum_v, value_weight))
    )
    out_shape = (seq_count, rows, width)
    return (
        block_out.reshape(out_shape),
        grad_hidden.reshape(out_shape),
        gain_attn / norm_gain_attn,
        sum_q,
        sum_k,
        sum_v,
        sum_out,
        sum_rest[:bucket_count, :head_count],
        sum_rest[bucket_count + expert_count],
        sum_router.T,
        grad_in,
        grad_out,
    )


def solution(mesh):
    placed = (
        P("wide", "narrow", None),
        P("wide"),
        P("wide", "narrow", None),
        P(),
        P(),
        P(),
        P(),
        P(),
        P(),
        P(),
        P(),
        P("wide", None, "narrow"),
        P("wide", "narrow", None),
        P("wide", "narrow", None),
    )
    return jax.shard_map(
        on_device,
        mesh=mesh,
        in_specs=placed,
        out_specs=(
            P("wide", "narrow", None),
            P("wide", "narrow", None),
            P(),
            P(),
            P(),
            P(),
            P(),
            P(),
            P(),
            P(),
            P("wide", None, "narrow"),
            P("wide", "narrow", None),
        ),
        check_vma=False,
    )
```

```python
import functools

import jax
import jax.numpy as jnp
import numpy as np
from jax import lax
from jax.experimental import pallas as pl
from jax.experimental.pallas import tpu as pltpu
from jax.sharding import PartitionSpec as P

epsilon = 1e-06
bucket_edges = (1, 2, 3, 4, 5, 6, 7, 8, 12, 16, 23, 32, 46, 64, 91)
LOG2E = 1.4426950408889634
LN2 = 0.6931471805599453
TILE = 128
VMEM_LIMIT = 56 * 1024 * 1024
NT = (((1,), (1,)), ((), ()))
NN = (((1,), (0,)), ((), ()))
TN = (((0,), (0,)), ((), ()))
BRIEF = pl.CostEstimate(flops=1, bytes_accessed=1, transcendentals=0)
LONG = pl.CostEstimate(flops=12_000_000_000, bytes_accessed=1, transcendentals=0)
BF16 = jnp.bfloat16
F32 = jnp.float32


def dotf(a, b, dims=NN):
    return lax.dot_general(a, b, dims, preferred_element_type=F32)


def rms_factor(values):
    return lax.rsqrt(jnp.mean(values * values, axis=-1, keepdims=True) + epsilon)


def rms_pull(values, factor, gain, grad):
    normal = values * factor
    scaled = grad * gain
    mean = jnp.mean(scaled * normal, axis=-1, keepdims=True)
    return (scaled - normal * mean) * factor, grad * normal


def bucket_of(offsets, bucket_count):
    magnitude = jnp.abs(offsets)
    bucket = jnp.zeros_like(offsets)
    for border in bucket_edges:
        bucket = bucket + (magnitude >= border).astype(jnp.int32)
    return bucket + bucket_count // 2 * (offsets > 0).astype(jnp.int32)


def pieces(x):
    hi = x.astype(BF16)
    rest = x - hi.astype(F32)
    mid = rest.astype(BF16)
    low = (rest - mid.astype(F32)).astype(BF16)
    return hi, mid, low


def tiles_kernel(rows, tiles):
    heads = tiles.shape[0]
    for h in range(heads):
        for d in range(3):
            values = jnp.broadcast_to(rows[h : h + 1, d * TILE : d * TILE + 2 * TILE], (TILE, 2 * TILE))
            moved = pltpu.roll(values, 0, 1, stride=1, stride_axis=0)[:, TILE:].T
            tiles[h, d] = moved
            if d == 0:
                tiles[h, 3] = moved - rows[h : h + 1, 4 * TILE : 5 * TILE]
            if d == 2:
                tiles[h, 4] = moved - rows[h : h + 1, 5 * TILE :]


def bias_tiles(bias_table):
    buckets, heads = bias_table.shape
    bucket = bucket_of(jnp.arange(4 * TILE, dtype=jnp.int32) - 2 * TILE, buckets)
    ends = jnp.repeat(jnp.array([buckets // 2 - 1, buckets - 1], jnp.int32), TILE)
    onehot = jnp.concatenate((bucket, ends))[None] == jnp.arange(buckets, dtype=jnp.int32)[:, None]
    rows = lax.dot_general(
        bias_table * LOG2E, onehot.astype(F32), TN, precision=lax.Precision.HIGHEST
    )
    return pl.pallas_call(
        tiles_kernel,
        out_shape=jax.ShapeDtypeStruct((heads, 5, TILE, TILE), F32),
        name="bias_tiles",
    )(rows)


def query_lanes(bias_table, rows):
    buckets, heads = bias_table.shape
    count = rows // TILE
    code = np.zeros((count, 128), np.int32)
    for lane in range(128):
        k = lane % 64
        for a in range(count):
            if 3 <= k < 9:
                code[a, lane] = k - 2
            elif 9 <= k < 9 + 3 * count:
                t = (k - 9) // 3
                code[a, lane] = 1 + k % 3 if t <= a - 2 else 4 + k % 3 if t >= a + 2 else 0
            elif k == 9 + 3 * count:
                code[a, lane] = 7
    values = pieces(bias_table[buckets // 2 - 1] * LOG2E) + pieces(bias_table[buckets - 1] * LOG2E)
    values = values + (jnp.ones((heads,), BF16),)
    code = jnp.asarray(np.repeat(code, TILE, axis=0))[None]
    lanes = jnp.zeros((heads, rows, 128), BF16)
    for i, value in enumerate(values):
        lanes = jnp.where(code == i + 1, value[:, None, None], lanes)
    return lanes


def key_lanes(me, lengths, rows):
    count = rows // TILE
    shape = (lengths.shape[0], 4, rows, 128)
    lane = lax.broadcasted_iota(jnp.int32, shape, 3) % 64
    place = lax.broadcasted_iota(jnp.int32, shape, 2)
    u = lax.broadcasted_iota(jnp.int32, shape, 1)
    block = me ^ u
    one = lane < 3
    one = one | ((lane >= 3) & (lane < 6) & (block < me))
    one = one | ((lane >= 6) & (lane < 9) & (block > me))
    one = one | ((u == 0) & (lane >= 9) & (lane < 9 + 3 * count) & ((lane - 9) // 3 == place // TILE))
    dead = block * rows + place >= lengths[:, None, None, None]
    masked = (lane == 9 + 3 * count) & dead
    return jnp.where(masked, -1e30, one.astype(F32)).astype(BF16)


def neighbour_flags(me):
    one, three = me ^ 1, me ^ 3
    return jnp.stack((one == me + 1, one == me - 1, three == me + 1, three == me - 1)).astype(F32)


def own_lanes(head, rows):
    lane = lax.broadcasted_iota(jnp.int32, (rows, 128), 1)
    return (lane < 64) if head == 0 else (lane >= 64)


def forward_kernel(flags, q, keys, values, klanes, qlanes, tiles, att, qaug, s_ref):
    rows = q.shape[1]
    count = rows // TILE
    one = jnp.ones((), BF16)
    queries, tops, outs = [], [], []
    for h in range(2):
        own = own_lanes(h, rows)
        qa = jnp.where(own, q[0], qlanes[h])
        top = None
        for u in range(4):
            scores = dotf(qa, jnp.where(own, keys[0, u], klanes[0, u]), NT)
            parts = [
                [scores[a * 128 : a * 128 + 128, t * 128 : t * 128 + 128] for t in range(count)]
                for a in range(count)
            ]
            if u == 0:
                for a in range(count):
                    for t in range(max(0, a - 1), min(count, a + 2)):
                        parts[a][t] = parts[a][t] + tiles[h, t - a + 1].T
            if u in (1, 3):
                parts[-1][0] = parts[-1][0] + tiles[h, 4].T * flags[u - 1]
                parts[0][-1] = parts[0][-1] + tiles[h, 3].T * flags[u]
            if u != 2:
                scores = jnp.concatenate([jnp.concatenate(row, axis=1) for row in parts], axis=0)
            s_ref[h, :, u * rows : (u + 1) * rows] = scores
            for t in range(count):
                x = scores[:, t * 128 : t * 128 + 128]
                top = x if top is None else jnp.maximum(top, x)
        queries.append(qa)
        tops.append(jnp.max(top, axis=1, keepdims=True))
    for h in range(2):
        own, qa, top = own_lanes(h, rows), queries[h], tops[h]
        total = None
        for u in range(4):
            weights = jnp.exp2(s_ref[h, :, u * rows : (u + 1) * rows] - top).astype(BF16)
            part = dotf(weights, jnp.where(own, values[0, u], one))
            total = part if total is None else total + part
        turned = pltpu.roll(total, 64, 1)
        outs.append(total / turned)
        hi, mid, low = pieces(top + jnp.log2(jnp.where(own, turned, total)))
        lane = lax.broadcasted_iota(jnp.int32, (rows, 128), 1) - (64 if h == 0 else 0)
        qaug[0, h] = jnp.where(
            lane == 0, -hi, jnp.where(lane == 1, -mid, jnp.where(lane == 2, -low, qa))
        )
    att[0] = jnp.where(own_lanes(0, rows), outs[0], outs[1]).astype(BF16)


def attend_forward(seq, cost, flags, q, keys, values, klanes, qlanes, tiles):
    rows, width = q.shape[1:]
    pairs = width // 128
    return pl.pallas_call(
        forward_kernel,
        grid=(pairs,),
        in_specs=[
            pl.BlockSpec(memory_space=pltpu.SMEM),
            pl.BlockSpec((1, rows, 128), lambda p: (seq, 0, p)),
            pl.BlockSpec((1, 4, rows, 128), lambda p: (0, 0, 0, p)),
            pl.BlockSpec((1, 4, rows, 128), lambda p: (0, 0, 0, p)),
            pl.BlockSpec((1, 4, rows, 128), lambda p: (seq, 0, 0, 0)),
            pl.BlockSpec((2, rows, 128), lambda p: (p, 0, 0)),
            pl.BlockSpec((2, 5, TILE, TILE), lambda p: (p, 0, 0, 0)),
        ],
        out_specs=[
            pl.BlockSpec((1, rows, 128), lambda p: (0, 0, p)),
            pl.BlockSpec((1, 2, rows, 128), lambda p: (0, p, 0, 0)),
        ],
        out_shape=[
            jax.ShapeDtypeStruct((1, rows, width), BF16),
            jax.ShapeDtypeStruct((1, 2 * pairs, rows, 128), BF16),
        ],
        scratch_shapes=[pltpu.VMEM((2, rows, 4 * rows), F32)],
        compiler_params=pltpu.CompilerParams(
            dimension_semantics=("arbitrary",), vmem_limit_bytes=VMEM_LIMIT
        ),
        cost_estimate=cost,
        name="attend_forward",
    )(flags, q, keys, values, klanes, qlanes, tiles)


def backward_kernel(flags, qaug, keys, values, att, do, klanes, tiles, dq, dkeys, dvalues, table):
    rows = do.shape[1]
    count = rows // TILE
    own0 = own_lanes(0, rows)
    prod = do[0].astype(F32) * att[0].astype(F32)
    one, zero = jnp.ones((), BF16), jnp.zeros((), BF16)
    turned = []
    for h in range(2):
        own = own_lanes(h, rows)
        qa = qaug[0, h]
        delta = jnp.sum(jnp.where(own, prod, 0.0), axis=1, keepdims=True)
        hi, mid, _ = pieces(jnp.broadcast_to(delta, (rows, 128)))
        lane = lax.broadcasted_iota(jnp.int32, (rows, 128), 1) - (64 if h == 0 else 0)
        doa = jnp.where(own, do[0], jnp.where(lane == 0, -hi, jnp.where(lane == 1, -mid, zero)))
        near = {}
        corner = {-1: None, 1: None}
        dqt = None
        for u in range(4):
            ka = jnp.where(own, keys[0, u], klanes[0, u])
            va = jnp.where(own, values[0, u], one)
            st = dotf(ka, qa, NT)
            if u == 0:
                strips = []
                for t in range(count):
                    row = []
                    for a in range(count):
                        x = st[t * 128 : t * 128 + 128, a * 128 : a * 128 + 128]
                        row.append(x + tiles[h, t - a + 1] if abs(t - a) <= 1 else x)
                    strips.append(jnp.concatenate(row, axis=1))
                st = jnp.concatenate(strips, axis=0)
            if u in (1, 3):
                after, before = flags[u - 1], flags[u]
                first = jnp.concatenate(
                    (st[:128, : rows - 128], st[:128, rows - 128 :] + tiles[h, 4] * after), axis=1
                )
                last = jnp.concatenate(
                    (st[rows - 128 :, :128] + tiles[h, 3] * before, st[rows - 128 :, 128:]), axis=1
                )
                st = jnp.concatenate((first, st[128 : rows - 128], last), axis=0)
            probs = jnp.exp2(st)
            ds = probs * dotf(va, doa, NT)
            probs_low, ds_low = probs.astype(BF16), ds.astype(BF16)
            if u == 0:
                for d in (-1, 0, 1):
                    for a in range(max(0, -d), min(count, count - d)):
                        t = a + d
                        x = ds[t * 128 : t * 128 + 128, a * 128 : a * 128 + 128]
                        near[d] = near[d] + x if d in near else x
            if u in (1, 3):
                for d, x in ((1, ds[:128, rows - 128 :] * after), (-1, ds[rows - 128 :, :128] * before)):
                    corner[d] = x if corner[d] is None else corner[d] + x
            dv = dotf(probs_low, doa).astype(BF16)
            dk = (dotf(ds_low, qa) * LN2).astype(BF16)
            if h == 0:
                dkeys[0, u], dvalues[0, u] = dk, dv
            else:
                dkeys[0, u] = jnp.where(own0, dkeys[0, u], dk)
                dvalues[0, u] = jnp.where(own0, dvalues[0, u], dv)
            part = dotf(ka.T, ds_low)
            dqt = part if dqt is None else dqt + part
        turned.append(dqt.T)
        group = lax.broadcasted_iota(jnp.int32, (TILE, TILE), 0) // 8 * 8
        upper = lax.broadcasted_iota(jnp.int32, (TILE, TILE), 1) >= group
        before, after = near[-1] + corner[-1], near[1] + corner[1]
        inner = (jnp.where(upper, near[0], before), jnp.where(upper, after, near[0]))
        for i, x in enumerate(inner):
            lined = x[:8]
            for g in range(1, TILE // 8):
                lined = lined + pltpu.roll(x[8 * g : 8 * g + 8], TILE - 8 * g, 1)
            table[0, h, 8 * i : 8 * i + 8, :] = lined
        outer = (jnp.where(upper, before, 0.0), jnp.where(upper, 0.0, after), corner[-1], corner[1])
        for i, x in enumerate(outer):
            table[0, h, 16 + i : 17 + i, :] = jnp.sum(x, axis=0, keepdims=True)
    dq[0] = (jnp.where(own0, turned[0], turned[1]) * 0.125).astype(BF16)
    for h in range(2):
        for a in range(count):
            rest = jnp.sum(turned[h][a * 128 : a * 128 + 128], axis=0, keepdims=True)
            table[0, h, 20 + a : 21 + a, :] = rest


def attend_backward(seq, flags, qaug, keys, values, att, do, klanes, tiles):
    rows, width = do.shape[1:]
    pairs = width // 128
    return pl.pallas_call(
        backward_kernel,
        grid=(pairs,),
        in_specs=[
            pl.BlockSpec(memory_space=pltpu.SMEM),
            pl.BlockSpec((1, 2, rows, 128), lambda p: (0, p, 0, 0)),
            pl.BlockSpec((1, 4, rows, 128), lambda p: (0, 0, 0, p)),
            pl.BlockSpec((1, 4, rows, 128), lambda p: (0, 0, 0, p)),
            pl.BlockSpec((1, rows, 128), lambda p: (0, 0, p)),
            pl.BlockSpec((1, rows, 128), lambda p: (seq, 0, p)),
            pl.BlockSpec((1, 4, rows, 128), lambda p: (seq, 0, 0, 0)),
            pl.BlockSpec((2, 5, TILE, TILE), lambda p: (p, 0, 0, 0)),
        ],
        out_specs=[
            pl.BlockSpec((1, rows, 128), lambda p: (0, 0, p)),
            pl.BlockSpec((1, 4, rows, 128), lambda p: (0, 0, 0, p)),
            pl.BlockSpec((1, 4, rows, 128), lambda p: (0, 0, 0, p)),
            pl.BlockSpec((1, 2, 32, 128), lambda p: (0, p, 0, 0)),
        ],
        out_shape=[
            jax.ShapeDtypeStruct((1, rows, width), BF16),
            jax.ShapeDtypeStruct((1, 4, rows, width), BF16),
            jax.ShapeDtypeStruct((1, 4, rows, width), BF16),
            jax.ShapeDtypeStruct((1, 2 * pairs, 32, 128), F32),
        ],
        compiler_params=pltpu.CompilerParams(
            dimension_semantics=("arbitrary",), vmem_limit_bytes=VMEM_LIMIT
        ),
        cost_estimate=BRIEF,
        name="attend_backward",
    )(flags, qaug, keys, values, att, do, klanes, tiles)


def table_grad(table, rows, bucket_count):
    count = rows // TILE
    heads = table.shape[0]
    row = jnp.arange(16, dtype=jnp.int32)[:, None]
    lane = jnp.arange(TILE, dtype=jnp.int32)[None, :]
    bucket = bucket_of(row // 8 * TILE + row % 8 - lane, bucket_count)
    ids = jnp.arange(bucket_count, dtype=jnp.int32)
    onehot = (bucket[None] == ids[:, None, None]).astype(F32)
    near = jnp.einsum("hil,bil->bh", table[:, :16], onehot, precision=lax.Precision.HIGHEST)
    halves = table[:, 20 : 20 + count].reshape(heads // 2, 2, count, 2, 64)
    rest = jnp.stack((halves[:, 0, :, 1], halves[:, 1, :, 0]), axis=1).reshape(heads, count, 64)
    outer = jnp.sum(table[:, 16:20], axis=2)
    left = jnp.sum(rest[:, :, 3], axis=1) + outer[:, 0] - outer[:, 2]
    right = jnp.sum(rest[:, :, 6], axis=1) + outer[:, 1] - outer[:, 3]
    for a in range(count):
        for t in range(count):
            if t <= a - 2:
                left = left + rest[:, a, 9 + 3 * t]
            if t >= a + 2:
                right = right + rest[:, a, 9 + 3 * t]
    far = jnp.where((ids == bucket_count // 2 - 1)[:, None], left[None, :], 0.0)
    return near + far + jnp.where((ids == bucket_count - 1)[:, None], right[None, :], 0.0)


def expert_kernel(experts, fresh, own, x, c, w0, w1, w2, w3, router, *refs):
    (hidden, grad_pre, low_c, back, grad_x, grad_logits) = refs[0 if fresh else 3 :][:6]
    gate_ref, probs_ref, out_acc, x_acc, w_in, w_out, sems = refs[-7:]
    step = pl.program_id(0)
    shards = (w0, w1, w2, w3)
    rows, width = x.shape

    def fetch(u):
        return (
            pltpu.make_async_copy(shards[u].at[pl.ds(0, width)], w_in.at[u], sems.at[0, u]),
            pltpu.make_async_copy(shards[u].at[pl.ds(width, width)], w_out.at[u], sems.at[1, u]),
        )

    for u in range(4):

        @pl.when(step == max(u - 1, 0))
        def _():
            for copy in fetch(u):
                copy.start()

    @pl.when(step == 0)
    def _():
        ids = lax.broadcasted_iota(jnp.int32, probs_ref.shape, 1)
        logits = jnp.where(ids < experts, dotf(x[...], router[...]), -1e30)
        weights = jnp.exp(logits - jnp.max(logits, axis=1, keepdims=True))
        probs = weights / jnp.sum(weights, axis=1, keepdims=True)
        probs_ref[...] = probs
        gate = jnp.sum(jnp.where(ids == own[0], probs, 0.0), axis=1, keepdims=True)
        gate_ref[...] = jnp.broadcast_to(gate, gate_ref.shape)
        low_c[...] = (c[...].astype(F32) * gate).astype(BF16)
        out_acc[...] = jnp.zeros_like(out_acc)
        x_acc[...] = jnp.zeros_like(x_acc)

    for u in range(4):

        @pl.when(step == u)
        def _():
            for copy in fetch(u):
                copy.wait()

    first, second = w_in[step], w_out[step]
    pre = dotf(x[...], first)
    units = dotf(low_c[...], second, NT)
    below = 0.5 + 0.5 * lax.erf(pre * 0.7071067811865476)
    hid = (pre * below).astype(BF16)
    slope = below + pre * (jnp.exp(pre * pre * -0.5) * 0.3989422804014327)
    low = (slope * units).astype(BF16)
    hidden[0] = hid
    grad_pre[0] = low
    out_acc[...] += dotf(hid, second)
    x_acc[...] += dotf(low, first, NT)

    @pl.when(step == 3)
    def _():
        result = out_acc[...]
        gate = gate_ref[:, :1]
        probs = probs_ref[...]
        grad_gate = jnp.sum(c[...].astype(F32) * result.astype(BF16).astype(F32), axis=1, keepdims=True)
        ids = lax.broadcasted_iota(jnp.int32, probs.shape, 1)
        mine = jnp.where(ids == own[0], 1.0, 0.0)
        logits = (grad_gate * probs * (mine - gate)).astype(BF16)
        grad_logits[...] = logits
        back[...] = (result * gate).astype(BF16)
        grad_x[...] = (x_acc[...] + dotf(logits, router[...], NT)).astype(BF16)


def run_expert(half, experts, own, x, c, shards, router, kept=()):
    rows, width = x.shape
    lanes = router.shape[1]
    whole = lambda u: (0, 0)
    anywhere = pl.BlockSpec(memory_space=pl.ANY)
    blocks = pl.BlockSpec((1, rows, width), lambda u: (u, half, 0))
    both = jax.ShapeDtypeStruct((4, 2 * rows, width), BF16)
    one = jax.ShapeDtypeStruct((rows, width), BF16)
    return pl.pallas_call(
        functools.partial(expert_kernel, experts, not kept),
        grid=(4,),
        in_specs=[
            pl.BlockSpec(memory_space=pltpu.SMEM),
            pl.BlockSpec((rows, width), whole),
            pl.BlockSpec((rows, width), whole),
        ]
        + [anywhere] * 4
        + [pl.BlockSpec((width, lanes), whole)]
        + [anywhere] * len(kept),
        out_specs=[blocks, blocks, pl.BlockSpec((rows, width), lambda u: (half, 0))]
        + [pl.BlockSpec((rows, width), whole)] * 2
        + [pl.BlockSpec((rows, lanes), whole)],
        out_shape=[both, both, jax.ShapeDtypeStruct((2 * rows, width), BF16), one, one]
        + [jax.ShapeDtypeStruct((rows, lanes), BF16)],
        scratch_shapes=[
            pltpu.VMEM((rows, 128), F32),
            pltpu.VMEM((rows, lanes), F32),
            pltpu.VMEM((rows, width), F32),
            pltpu.VMEM((rows, width), F32),
            pltpu.VMEM((4, width, width), BF16),
            pltpu.VMEM((4, width, width), BF16),
            pltpu.SemaphoreType.DMA((2, 4)),
        ],
        input_output_aliases={8 + i: i for i in range(len(kept))},
        compiler_params=pltpu.CompilerParams(
            dimension_semantics=("arbitrary",), vmem_limit_bytes=VMEM_LIMIT
        ),
        cost_estimate=BRIEF,
        name="run_expert",
    )(own, x, c, *shards, router, *kept)


def swap(x, bit):
    return lax.ppermute(x, "narrow", [(i, i ^ bit) for i in range(4)])


def swap_wide(x, bit):
    return lax.ppermute(x, "wide", [(i, i ^ bit) for i in range(lax.axis_size("wide"))])


def after(x, *others):
    return lax.optimization_barrier((x,) + others)[0]


def pick(x, index):
    return lax.dynamic_index_in_dim(x, index, 0, keepdims=False)


def scatter_first(blocks):
    half = blocks.shape[1] // 2
    return swap(blocks[3, :half], 1), swap(blocks[3, half:], 2)


def scatter_second(blocks, from_one, from_two):
    half = blocks.shape[1] // 2
    one = jnp.concatenate(
        (blocks[1, :half], (blocks[1, half:].astype(F32) + from_two.astype(F32)).astype(BF16)), axis=0
    )
    two = jnp.concatenate(
        ((blocks[2, :half].astype(F32) + from_one.astype(F32)).astype(BF16), blocks[2, half:]), axis=0
    )
    return swap(one, 1), swap(two, 2)


def sum_everywhere(x, beside):
    wide = lax.axis_index("wide")
    narrow = lax.axis_index("narrow")
    layers = lax.axis_size("wide") // 2
    rows = x.shape[0]
    x = jnp.pad(x.astype(BF16), ((0, -rows % (8 * layers)), (0, 0)))

    def layer_swap(a, k):
        return swap_wide(a, 2 * k)

    levels = ((2, wide % 2, swap_wide), (4, narrow, swap), (layers, wide // 2, layer_swap))
    for step, (count, place, send) in enumerate(levels):
        x = beside(step, x).reshape(count, x.shape[0] // count, -1)
        total = pick(x, place).astype(F32)
        for k in range(1, count):
            total = total + send(pick(x, place ^ k), k).astype(F32)
        x = total.astype(BF16)
    for step, (count, place, send) in enumerate(reversed(levels)):
        x = beside(3 + step, x)
        parts = jnp.stack([x] + [send(x, k) for k in range(1, count)])
        x = jnp.concatenate([pick(parts, place ^ i) for i in range(count)], axis=0)
    return x[:rows]


def on_device(
    hidden_in,
    lengths,
    routes,
    norm_gain_attn,
    query_weight,
    key_weight,
    value_weight,
    out_weight,
    bias_table,
    norm_gain_ffn,
    router_weight,
    expert_in,
    expert_out,
    cotangent,
):
    wide_count = lax.axis_size("wide")
    seq_count, rows, width = hidden_in.shape
    bucket_count, head_count = bias_table.shape
    pairs = width // 128
    tokens = seq_count * rows
    local_experts = expert_in.shape[0]
    expert_count = local_experts * wide_count
    capacity = 5 * tokens // (4 * expert_count)
    slots = wide_count * capacity
    me = lax.axis_index("narrow")
    near = me // 2
    far = 1 - near
    own = jnp.reshape(lax.axis_index("wide") * local_experts + near, (1,))

    source = hidden_in.astype(F32).reshape(tokens, width)
    factor_attn = rms_factor(source)
    normed = (source * factor_attn * norm_gain_attn).astype(BF16)
    normed_seqs = normed.reshape(seq_count, rows, width)
    queries = (dotf(normed, query_weight) * (LOG2E / 8)).astype(BF16).reshape(seq_count, rows, width)
    flags = neighbour_flags(me)
    klanes = key_lanes(me, lengths, rows)
    qlanes = query_lanes(bias_table, rows)
    tiles = bias_tiles(bias_table)
    router = jnp.pad(router_weight, ((0, 0), (0, -expert_count % 128)))
    shards = [
        jnp.concatenate((pick(expert_in, e), pick(expert_out, e)), axis=0) for e in (near, far)
    ]

    blocks = []
    for s in range(seq_count):
        mine = after(normed_seqs[s], *others) if s else normed_seqs[s]
        others = [swap(mine, u) for u in range(1, 4)]
        if s == 0:
            first = (others, queries, klanes, qlanes, tiles, shards)
            first = lax.optimization_barrier(first)
            first, queries, klanes, qlanes, tiles, shards = first
        blocks.append(jnp.stack([mine] + (others if s else first)))

    route = routes.reshape(tokens)
    position = me * rows + jnp.arange(rows, dtype=jnp.int32)
    live = (position[None, :] < lengths[:, None]).reshape(tokens)
    expert_ids = jnp.arange(expert_count, dtype=jnp.int32)
    chosen = ((route[:, None] == expert_ids[None, :]) & live[:, None]).astype(F32)
    token_ids = jnp.arange(tokens, dtype=jnp.int32)
    earlier = (token_ids[:, None] > token_ids[None, :]).astype(BF16)
    place = jnp.sum(dotf(earlier, chosen.astype(BF16)) * chosen, axis=-1).astype(jnp.int32)
    kept = live & (place < capacity)
    slot = route // local_experts * capacity + place
    slot_ids = jnp.arange(slots, dtype=jnp.int32)

    def slot_map(expert):
        due = jnp.where(kept & (route % local_experts == expert), slot, -1)
        return (slot_ids[:, None] == due[None, :]).astype(BF16)

    map_far, map_near = slot_map(far), slot_map(near)

    def exchange(values):
        sent = values.reshape(wide_count, -1, width)
        return lax.all_to_all(sent, "wide", 0, 0, tiled=True)

    cot = cotangent.reshape(tokens, width)
    cot_far = dotf(map_far, cot).astype(BF16).reshape(wide_count, capacity, width)
    cot_near = dotf(map_near, cot).astype(BF16).reshape(wide_count, capacity, width)
    got = exchange(jnp.concatenate((cot_far, cot_near), axis=1).reshape(2 * slots, width))
    cot_far = swap(got[:, :capacity].reshape(slots, width), 2)
    cot_near = got[:, capacity:].reshape(slots, width)

    kvs, atts, qaugs = [], [], []
    for s in range(seq_count):
        rows_all = blocks[s].reshape(4 * rows, width)
        kvs.append(
            [
                dotf(rows_all, w).astype(BF16).reshape(1, 4, rows, width)
                for w in (key_weight, value_weight)
            ]
        )
        cost = LONG if s == 0 else BRIEF
        att, qaug = attend_forward(s, cost, flags, queries, *kvs[s], klanes, qlanes, tiles)
        atts.append(att)
        qaugs.append(qaug)
        if s == 0:
            shards, _ = lax.optimization_barrier((shards, att))
            shards = [shards[0], swap(shards[0], 1), swap(shards[1], 2)]
    attended = jnp.concatenate(atts, axis=0).reshape(tokens, width)
    attended, shards = lax.optimization_barrier((attended, shards))
    shards.append(swap(shards[2], 1))
    residual = source + dotf(attended, out_weight)
    factor_ffn = rms_factor(residual)
    ffn_input = (residual * factor_ffn * norm_gain_ffn).astype(BF16)

    sent_far = dotf(map_far, ffn_input).astype(BF16)
    sent_near = dotf(map_near, after(ffn_input, sent_far)).astype(BF16)
    x_far = swap(exchange(sent_far).reshape(slots, width), 2)
    x_near = exchange(sent_near).reshape(slots, width)
    *shared, back_far, grad_x_far, logits_far = run_expert(
        0, expert_count, own, x_far, cot_far, shards, router
    )
    grad_x_far = swap(grad_x_far, 2)
    hidden, grad_pre, low_c, back_near, grad_x_near, logits_near = run_expert(
        1, expert_count, own, x_near, cot_near, shards, router, tuple(shared)
    )
    sent = jnp.concatenate(
        [x.reshape(wide_count, capacity, width) for x in (grad_x_far, grad_x_near)], axis=1
    )
    got = exchange(sent)

    x_far, x_near, low_c, logits_far, logits_near, _ = lax.optimization_barrier(
        (x_far, x_near, low_c, logits_far, logits_near, sent)
    )
    xs = jnp.concatenate((x_far, x_near), axis=0)
    grad_experts = [None] * 4
    for u in (3, 1, 2, 0):
        both = (dotf(xs, grad_pre[u], TN), dotf(hidden[u], low_c, TN))
        both = jnp.concatenate([x.astype(BF16) for x in both], axis=0)
        grad_experts[u] = swap(both, u) if u else both
    back_far = swap(after(back_far, sent), 2)
    got, grad_experts[0] = lax.optimization_barrier((got, grad_experts[0]))
    grad_x_far, grad_x_near = (
        x.reshape(slots, width) for x in (got[:, :capacity], got[:, capacity:])
    )

    grad_router = dotf(x_far, logits_far, TN) + dotf(x_near, logits_near, TN)

    grad_ffn_input = dotf(map_near, grad_x_near, TN) + dotf(map_far, grad_x_far, TN)
    grad_norm, gain_ffn = rms_pull(residual, factor_ffn, norm_gain_ffn, grad_ffn_input)
    gain_ffn = jnp.sum(gain_ffn, axis=0)
    grad_residual = cot.astype(F32) + grad_norm
    grad_branch = grad_residual.astype(BF16)
    grad_out_weight = dotf(attended, grad_branch, TN)
    grad_attended = dotf(grad_branch, out_weight, NT).astype(BF16).reshape(seq_count, rows, width)
    back = jnp.concatenate(
        [x.reshape(wide_count, capacity, width) for x in (back_far, back_near)], axis=1
    )
    grad_attended, back = lax.optimization_barrier((grad_attended, back))
    back = exchange(back)
    def normed_blocks(s):
        part = dotf(dks[s], key_weight, NT) + dotf(dvs[s], value_weight, NT)
        return part.astype(BF16).reshape(4, rows, width)

    dqs, dks, dvs = [], [], []
    table = 0.0
    for s in range(seq_count):
        dq, dk, dv, table_one = attend_backward(
            s, flags, qaugs[s], *kvs[s], atts[s], grad_attended, klanes, tiles
        )
        dqs.append(dq.reshape(rows, width))
        dks.append(dk.reshape(4 * rows, width))
        dvs.append(dv.reshape(4 * rows, width))
        table = table + table_one[0]
        if s == 0:
            parts = normed_blocks(0)
            grad_attended, parts = lax.optimization_barrier((grad_attended, parts))
            halves = scatter_first(parts)
    dqs, dks, dvs, grad_experts, back, halves = lax.optimization_barrier(
        (dqs, dks, dvs, grad_experts, back, halves)
    )
    scattered = [scatter_second(parts, *halves)]
    ours = [parts[0]]
    summands = [
        sum(dotf(x.reshape(-1, width), g, TN) for x, g in zip(xs, grads))
        for xs, grads in ((normed_seqs, dqs), (blocks, dks), (blocks, dvs))
    ]
    table = table_grad(table, rows, bucket_count)
    rest = jnp.concatenate(
        (
            jnp.pad(table, ((0, 0), (0, width - head_count))),
            grad_router.T[:expert_count],
            gain_ffn[None],
            jnp.zeros((-(bucket_count + expert_count + 1) % 64, width), F32),
        ),
        axis=0,
    )
    summands = [x.astype(BF16) for x in summands + [grad_out_weight, rest]]
    summands, dqs, dks, dvs = lax.optimization_barrier((summands, dqs, dks, dvs))

    def beside(step, x):
        nonlocal halves, grad_experts, back
        if step == 1:
            ours.append(normed_blocks(1))
            x, ours[1], scattered[0] = lax.optimization_barrier((x, ours[1], scattered[0]))
            halves = scatter_first(ours[1])
        if step == 2:
            x, halves, grad_experts, back = lax.optimization_barrier(
                (x, halves, grad_experts, back)
            )
            scattered.append(scatter_second(ours[1], *halves))
            ours[1] = ours[1][0]
        if step == 4:
            x, scattered[1] = lax.optimization_barrier((x, scattered[1]))
        return x

    sums = sum_everywhere(jnp.concatenate(summands, axis=0), beside).astype(F32)
    block_out = residual + dotf(map_far, back[:, :capacity].reshape(slots, width), TN)
    block_out = block_out + dotf(map_near, back[:, capacity:].reshape(slots, width), TN)
    zero, one, two, three = (x.astype(F32).reshape(2, 1, width, -1) for x in grad_experts)
    zero, other = zero + one, two + three
    grad_in, grad_out = jnp.where(
        near == 0, jnp.concatenate((zero, other), axis=1), jnp.concatenate((other, zero), axis=1)
    )

    grad_normed = jnp.concatenate(
        [
            mine.astype(F32) + sum(x.astype(F32) for x in arrived) + dotf(dq, query_weight, NT)
            for mine, arrived, dq in zip(ours, scattered, dqs)
        ],
        axis=0,
    )
    grad_hidden = grad_residual + rms_pull(source, factor_attn, norm_gain_attn, grad_normed)[0]

    sum_q, sum_k, sum_v, sum_out = (sums[i * width : (i + 1) * width] for i in range(4))
    sum_rest = sums[4 * width :]
    sum_router = sum_rest[bucket_count : bucket_count + expert_count]
    gain_attn = jnp.sum(
        sum_q * query_weight.astype(F32)
        + sum_k * key_weight.astype(F32)
        + sum_v * value_weight.astype(F32),
        axis=1,
    )
    out_shape = (seq_count, rows, width)
    return (
        block_out.reshape(out_shape),
        grad_hidden.reshape(out_shape),
        gain_attn / norm_gain_attn,
        sum_q,
        sum_k,
        sum_v,
        sum_out,
        sum_rest[:bucket_count, :head_count],
        sum_rest[bucket_count + expert_count],
        sum_router.T,
        grad_in,
        grad_out,
    )


def solution(mesh):
    placed = (
        P("wide", "narrow", None),
        P("wide"),
        P("wide", "narrow", None),
        P(),
        P(),
        P(),
        P(),
        P(),
        P(),
        P(),
        P(),
        P("wide", None, "narrow"),
        P("wide", "narrow", None),
        P("wide", "narrow", None),
    )
    return jax.shard_map(
        on_device,
        mesh=mesh,
        in_specs=placed,
        out_specs=(
            P("wide", "narrow", None),
            P("wide", "narrow", None),
            P(),
            P(),
            P(),
            P(),
            P(),
            P(),
            P(),
            P(),
            P("wide", None, "narrow"),
            P("wide", "narrow", None),
        ),
        check_vma=False,
    )
```

```python
import functools

import jax
import jax.numpy as jnp
import numpy as np
from jax import lax
from jax.experimental import pallas as pl
from jax.experimental.pallas import tpu as pltpu
from jax.sharding import PartitionSpec as P

epsilon = 1e-06
bucket_edges = (1, 2, 3, 4, 5, 6, 7, 8, 12, 16, 23, 32, 46, 64, 91)
LOG2E = 1.4426950408889634
LN2 = 0.6931471805599453
TILE = 128
VMEM_LIMIT = 56 * 1024 * 1024
NT = (((1,), (1,)), ((), ()))
NN = (((1,), (0,)), ((), ()))
TN = (((0,), (0,)), ((), ()))
BRIEF = pl.CostEstimate(flops=1, bytes_accessed=1, transcendentals=0)
LONG = pl.CostEstimate(flops=12_000_000_000, bytes_accessed=1, transcendentals=0)
BF16 = jnp.bfloat16
F32 = jnp.float32


def dotf(a, b, dims=NN):
    return lax.dot_general(a, b, dims, preferred_element_type=F32)


def rms_factor(values):
    return lax.rsqrt(jnp.mean(values * values, axis=-1, keepdims=True) + epsilon)


def rms_pull(values, factor, gain, grad):
    normal = values * factor
    scaled = grad * gain
    mean = jnp.mean(scaled * normal, axis=-1, keepdims=True)
    return (scaled - normal * mean) * factor, grad * normal


def bucket_of(offsets, bucket_count):
    magnitude = jnp.abs(offsets)
    bucket = jnp.zeros_like(offsets)
    for border in bucket_edges:
        bucket = bucket + (magnitude >= border).astype(jnp.int32)
    return bucket + bucket_count // 2 * (offsets > 0).astype(jnp.int32)


def pieces(x):
    hi = x.astype(BF16)
    rest = x - hi.astype(F32)
    mid = rest.astype(BF16)
    low = (rest - mid.astype(F32)).astype(BF16)
    return hi, mid, low


def tiles_kernel(rows, tiles):
    heads = tiles.shape[0]
    for h in range(heads):
        for d in range(3):
            values = jnp.broadcast_to(rows[h : h + 1, d * TILE : d * TILE + 2 * TILE], (TILE, 2 * TILE))
            moved = pltpu.roll(values, 0, 1, stride=1, stride_axis=0)[:, TILE:].T
            tiles[h, d] = moved
            if d == 0:
                tiles[h, 3] = moved - rows[h : h + 1, 4 * TILE : 5 * TILE]
            if d == 2:
                tiles[h, 4] = moved - rows[h : h + 1, 5 * TILE :]


def bias_tiles(bias_table):
    buckets, heads = bias_table.shape
    bucket = bucket_of(jnp.arange(4 * TILE, dtype=jnp.int32) - 2 * TILE, buckets)
    ends = jnp.repeat(jnp.array([buckets // 2 - 1, buckets - 1], jnp.int32), TILE)
    onehot = jnp.concatenate((bucket, ends))[None] == jnp.arange(buckets, dtype=jnp.int32)[:, None]
    rows = lax.dot_general(
        bias_table * LOG2E, onehot.astype(F32), TN, precision=lax.Precision.HIGHEST
    )
    return pl.pallas_call(
        tiles_kernel,
        out_shape=jax.ShapeDtypeStruct((heads, 5, TILE, TILE), F32),
        name="bias_tiles",
    )(rows)


def query_lanes(bias_table, rows):
    buckets, heads = bias_table.shape
    count = rows // TILE
    code = np.zeros((count, 128), np.int32)
    for lane in range(128):
        k = lane % 64
        for a in range(count):
            if 3 <= k < 9:
                code[a, lane] = k - 2
            elif 9 <= k < 9 + 3 * count:
                t = (k - 9) // 3
                code[a, lane] = 1 + k % 3 if t <= a - 2 else 4 + k % 3 if t >= a + 2 else 0
            elif k == 9 + 3 * count:
                code[a, lane] = 7
    values = pieces(bias_table[buckets // 2 - 1] * LOG2E) + pieces(bias_table[buckets - 1] * LOG2E)
    values = values + (jnp.ones((heads,), BF16),)
    code = jnp.asarray(np.repeat(code, TILE, axis=0))[None]
    lanes = jnp.zeros((heads, rows, 128), BF16)
    for i, value in enumerate(values):
        lanes = jnp.where(code == i + 1, value[:, None, None], lanes)
    return lanes


def key_lanes(me, lengths, rows):
    count = rows // TILE
    shape = (lengths.shape[0], 4, rows, 128)
    lane = lax.broadcasted_iota(jnp.int32, shape, 3) % 64
    place = lax.broadcasted_iota(jnp.int32, shape, 2)
    u = lax.broadcasted_iota(jnp.int32, shape, 1)
    block = me ^ u
    one = lane < 3
    one = one | ((lane >= 3) & (lane < 6) & (block < me))
    one = one | ((lane >= 6) & (lane < 9) & (block > me))
    one = one | ((u == 0) & (lane >= 9) & (lane < 9 + 3 * count) & ((lane - 9) // 3 == place // TILE))
    dead = block * rows + place >= lengths[:, None, None, None]
    masked = (lane == 9 + 3 * count) & dead
    return jnp.where(masked, -1e30, one.astype(F32)).astype(BF16)


def neighbour_flags(me):
    one, three = me ^ 1, me ^ 3
    return jnp.stack((one == me + 1, one == me - 1, three == me + 1, three == me - 1)).astype(F32)


def own_lanes(head, rows):
    lane = lax.broadcasted_iota(jnp.int32, (rows, 128), 1)
    return (lane < 64) if head == 0 else (lane >= 64)


def forward_kernel(flags, q, keys, values, klanes, qlanes, tiles, att, qaug, s_ref):
    rows = q.shape[1]
    count = rows // TILE
    one = jnp.ones((), BF16)
    queries, tops, outs = [], [], []
    for h in range(2):
        own = own_lanes(h, rows)
        qa = jnp.where(own, q[0], qlanes[h])
        top = None
        for u in range(4):
            scores = dotf(qa, jnp.where(own, keys[0, u], klanes[0, u]), NT)
            parts = [
                [scores[a * 128 : a * 128 + 128, t * 128 : t * 128 + 128] for t in range(count)]
                for a in range(count)
            ]
            if u == 0:
                for a in range(count):
                    for t in range(max(0, a - 1), min(count, a + 2)):
                        parts[a][t] = parts[a][t] + tiles[h, t - a + 1].T
            if u in (1, 3):
                parts[-1][0] = parts[-1][0] + tiles[h, 4].T * flags[u - 1]
                parts[0][-1] = parts[0][-1] + tiles[h, 3].T * flags[u]
            if u != 2:
                scores = jnp.concatenate([jnp.concatenate(row, axis=1) for row in parts], axis=0)
            s_ref[h, :, u * rows : (u + 1) * rows] = scores
            for t in range(count):
                x = scores[:, t * 128 : t * 128 + 128]
                top = x if top is None else jnp.maximum(top, x)
        queries.append(qa)
        tops.append(jnp.max(top, axis=1, keepdims=True))
    for h in range(2):
        own, qa, top = own_lanes(h, rows), queries[h], tops[h]
        total = None
        for u in range(4):
            weights = jnp.exp2(s_ref[h, :, u * rows : (u + 1) * rows] - top).astype(BF16)
            part = dotf(weights, jnp.where(own, values[0, u], one))
            total = part if total is None else total + part
        turned = pltpu.roll(total, 64, 1)
        outs.append(total / turned)
        hi, mid, low = pieces(top + jnp.log2(jnp.where(own, turned, total)))
        lane = lax.broadcasted_iota(jnp.int32, (rows, 128), 1) - (64 if h == 0 else 0)
        qaug[0, h] = jnp.where(
            lane == 0, -hi, jnp.where(lane == 1, -mid, jnp.where(lane == 2, -low, qa))
        )
    att[0] = jnp.where(own_lanes(0, rows), outs[0], outs[1]).astype(BF16)


def attend_forward(seq, cost, flags, q, keys, values, klanes, qlanes, tiles):
    rows, width = q.shape[1:]
    pairs = width // 128
    return pl.pallas_call(
        forward_kernel,
        grid=(pairs,),
        in_specs=[
            pl.BlockSpec(memory_space=pltpu.SMEM),
            pl.BlockSpec((1, rows, 128), lambda p: (seq, 0, p)),
            pl.BlockSpec((1, 4, rows, 128), lambda p: (0, 0, 0, p)),
            pl.BlockSpec((1, 4, rows, 128), lambda p: (0, 0, 0, p)),
            pl.BlockSpec((1, 4, rows, 128), lambda p: (seq, 0, 0, 0)),
            pl.BlockSpec((2, rows, 128), lambda p: (p, 0, 0)),
            pl.BlockSpec((2, 5, TILE, TILE), lambda p: (p, 0, 0, 0)),
        ],
        out_specs=[
            pl.BlockSpec((1, rows, 128), lambda p: (0, 0, p)),
            pl.BlockSpec((1, 2, rows, 128), lambda p: (0, p, 0, 0)),
        ],
        out_shape=[
            jax.ShapeDtypeStruct((1, rows, width), BF16),
            jax.ShapeDtypeStruct((1, 2 * pairs, rows, 128), BF16),
        ],
        scratch_shapes=[pltpu.VMEM((2, rows, 4 * rows), F32)],
        compiler_params=pltpu.CompilerParams(
            dimension_semantics=("arbitrary",), vmem_limit_bytes=VMEM_LIMIT
        ),
        cost_estimate=cost,
        name="attend_forward",
    )(flags, q, keys, values, klanes, qlanes, tiles)


def backward_kernel(flags, qaug, keys, values, att, do, klanes, tiles, dq, dkeys, dvalues, table):
    rows = do.shape[1]
    count = rows // TILE
    own0 = own_lanes(0, rows)
    prod = do[0].astype(F32) * att[0].astype(F32)
    one, zero = jnp.ones((), BF16), jnp.zeros((), BF16)
    turned = []
    for h in range(2):
        own = own_lanes(h, rows)
        qa = qaug[0, h]
        delta = jnp.sum(jnp.where(own, prod, 0.0), axis=1, keepdims=True)
        hi, mid, _ = pieces(jnp.broadcast_to(delta, (rows, 128)))
        lane = lax.broadcasted_iota(jnp.int32, (rows, 128), 1) - (64 if h == 0 else 0)
        doa = jnp.where(own, do[0], jnp.where(lane == 0, -hi, jnp.where(lane == 1, -mid, zero)))
        near = {}
        corner = {-1: None, 1: None}
        dqt = None
        for u in range(4):
            ka = jnp.where(own, keys[0, u], klanes[0, u])
            va = jnp.where(own, values[0, u], one)
            st = dotf(ka, qa, NT)
            if u == 0:
                strips = []
                for t in range(count):
                    row = []
                    for a in range(count):
                        x = st[t * 128 : t * 128 + 128, a * 128 : a * 128 + 128]
                        row.append(x + tiles[h, t - a + 1] if abs(t - a) <= 1 else x)
                    strips.append(jnp.concatenate(row, axis=1))
                st = jnp.concatenate(strips, axis=0)
            if u in (1, 3):
                after, before = flags[u - 1], flags[u]
                first = jnp.concatenate(
                    (st[:128, : rows - 128], st[:128, rows - 128 :] + tiles[h, 4] * after), axis=1
                )
                last = jnp.concatenate(
                    (st[rows - 128 :, :128] + tiles[h, 3] * before, st[rows - 128 :, 128:]), axis=1
                )
                st = jnp.concatenate((first, st[128 : rows - 128], last), axis=0)
            probs = jnp.exp2(st)
            ds = probs * dotf(va, doa, NT)
            probs_low, ds_low = probs.astype(BF16), ds.astype(BF16)
            if u == 0:
                for d in (-1, 0, 1):
                    for a in range(max(0, -d), min(count, count - d)):
                        t = a + d
                        x = ds[t * 128 : t * 128 + 128, a * 128 : a * 128 + 128]
                        near[d] = near[d] + x if d in near else x
            if u in (1, 3):
                for d, x in ((1, ds[:128, rows - 128 :] * after), (-1, ds[rows - 128 :, :128] * before)):
                    corner[d] = x if corner[d] is None else corner[d] + x
            dv = dotf(probs_low, doa).astype(BF16)
            dk = (dotf(ds_low, qa) * LN2).astype(BF16)
            if h == 0:
                dkeys[0, u], dvalues[0, u] = dk, dv
            else:
                dkeys[0, u] = jnp.where(own0, dkeys[0, u], dk)
                dvalues[0, u] = jnp.where(own0, dvalues[0, u], dv)
            part = dotf(ka.T, ds_low)
            dqt = part if dqt is None else dqt + part
        turned.append(dqt.T)
        group = lax.broadcasted_iota(jnp.int32, (TILE, TILE), 0) // 8 * 8
        upper = lax.broadcasted_iota(jnp.int32, (TILE, TILE), 1) >= group
        before, after = near[-1] + corner[-1], near[1] + corner[1]
        inner = (jnp.where(upper, near[0], before), jnp.where(upper, after, near[0]))
        for i, x in enumerate(inner):
            lined = x[:8]
            for g in range(1, TILE // 8):
                lined = lined + pltpu.roll(x[8 * g : 8 * g + 8], TILE - 8 * g, 1)
            table[0, h, 8 * i : 8 * i + 8, :] = lined
        outer = (jnp.where(upper, before, 0.0), jnp.where(upper, 0.0, after), corner[-1], corner[1])
        for i, x in enumerate(outer):
            table[0, h, 16 + i : 17 + i, :] = jnp.sum(x, axis=0, keepdims=True)
    dq[0] = (jnp.where(own0, turned[0], turned[1]) * 0.125).astype(BF16)
    for h in range(2):
        for a in range(count):
            rest = jnp.sum(turned[h][a * 128 : a * 128 + 128], axis=0, keepdims=True)
            table[0, h, 20 + a : 21 + a, :] = rest


def attend_backward(seq, flags, qaug, keys, values, att, do, klanes, tiles):
    rows, width = do.shape[1:]
    pairs = width // 128
    return pl.pallas_call(
        backward_kernel,
        grid=(pairs,),
        in_specs=[
            pl.BlockSpec(memory_space=pltpu.SMEM),
            pl.BlockSpec((1, 2, rows, 128), lambda p: (0, p, 0, 0)),
            pl.BlockSpec((1, 4, rows, 128), lambda p: (0, 0, 0, p)),
            pl.BlockSpec((1, 4, rows, 128), lambda p: (0, 0, 0, p)),
            pl.BlockSpec((1, rows, 128), lambda p: (0, 0, p)),
            pl.BlockSpec((1, rows, 128), lambda p: (seq, 0, p)),
            pl.BlockSpec((1, 4, rows, 128), lambda p: (seq, 0, 0, 0)),
            pl.BlockSpec((2, 5, TILE, TILE), lambda p: (p, 0, 0, 0)),
        ],
        out_specs=[
            pl.BlockSpec((1, rows, 128), lambda p: (0, 0, p)),
            pl.BlockSpec((1, 4, rows, 128), lambda p: (0, 0, 0, p)),
            pl.BlockSpec((1, 4, rows, 128), lambda p: (0, 0, 0, p)),
            pl.BlockSpec((1, 2, 32, 128), lambda p: (0, p, 0, 0)),
        ],
        out_shape=[
            jax.ShapeDtypeStruct((1, rows, width), BF16),
            jax.ShapeDtypeStruct((1, 4, rows, width), BF16),
            jax.ShapeDtypeStruct((1, 4, rows, width), BF16),
            jax.ShapeDtypeStruct((1, 2 * pairs, 32, 128), F32),
        ],
        compiler_params=pltpu.CompilerParams(
            dimension_semantics=("arbitrary",), vmem_limit_bytes=VMEM_LIMIT
        ),
        cost_estimate=BRIEF,
        name="attend_backward",
    )(flags, qaug, keys, values, att, do, klanes, tiles)


def table_grad(table, rows, bucket_count):
    count = rows // TILE
    heads = table.shape[0]
    row = jnp.arange(16, dtype=jnp.int32)[:, None]
    lane = jnp.arange(TILE, dtype=jnp.int32)[None, :]
    bucket = bucket_of(row // 8 * TILE + row % 8 - lane, bucket_count)
    ids = jnp.arange(bucket_count, dtype=jnp.int32)
    onehot = (bucket[None] == ids[:, None, None]).astype(F32)
    near = jnp.einsum("hil,bil->bh", table[:, :16], onehot, precision=lax.Precision.HIGHEST)
    halves = table[:, 20 : 20 + count].reshape(heads // 2, 2, count, 2, 64)
    rest = jnp.stack((halves[:, 0, :, 1], halves[:, 1, :, 0]), axis=1).reshape(heads, count, 64)
    outer = jnp.sum(table[:, 16:20], axis=2)
    left = jnp.sum(rest[:, :, 3], axis=1) + outer[:, 0] - outer[:, 2]
    right = jnp.sum(rest[:, :, 6], axis=1) + outer[:, 1] - outer[:, 3]
    for a in range(count):
        for t in range(count):
            if t <= a - 2:
                left = left + rest[:, a, 9 + 3 * t]
            if t >= a + 2:
                right = right + rest[:, a, 9 + 3 * t]
    far = jnp.where((ids == bucket_count // 2 - 1)[:, None], left[None, :], 0.0)
    return near + far + jnp.where((ids == bucket_count - 1)[:, None], right[None, :], 0.0)


def expert_kernel(experts, fresh, own, x, c, w0, w1, w2, w3, router, *refs):
    (hidden, grad_pre, low_c, back, grad_x, grad_logits) = refs[0 if fresh else 3 :][:6]
    gate_ref, probs_ref, out_acc, x_acc, w_in, w_out, sems = refs[-7:]
    step = pl.program_id(0)
    shards = (w0, w1, w2, w3)
    rows, width = x.shape

    def fetch(u):
        return (
            pltpu.make_async_copy(shards[u].at[pl.ds(0, width)], w_in.at[u], sems.at[0, u]),
            pltpu.make_async_copy(shards[u].at[pl.ds(width, width)], w_out.at[u], sems.at[1, u]),
        )

    for u in range(4):

        @pl.when(step == max(u - 1, 0))
        def _():
            for copy in fetch(u):
                copy.start()

    @pl.when(step == 0)
    def _():
        ids = lax.broadcasted_iota(jnp.int32, probs_ref.shape, 1)
        logits = jnp.where(ids < experts, dotf(x[...], router[...]), -1e30)
        weights = jnp.exp(logits - jnp.max(logits, axis=1, keepdims=True))
        probs = weights / jnp.sum(weights, axis=1, keepdims=True)
        probs_ref[...] = probs
        gate = jnp.sum(jnp.where(ids == own[0], probs, 0.0), axis=1, keepdims=True)
        gate_ref[...] = jnp.broadcast_to(gate, gate_ref.shape)
        low_c[...] = (c[...].astype(F32) * gate).astype(BF16)
        out_acc[...] = jnp.zeros_like(out_acc)
        x_acc[...] = jnp.zeros_like(x_acc)

    for u in range(4):

        @pl.when(step == u)
        def _():
            for copy in fetch(u):
                copy.wait()

    first, second = w_in[step], w_out[step]
    pre = dotf(x[...], first)
    units = dotf(low_c[...], second, NT)
    below = 0.5 + 0.5 * lax.erf(pre * 0.7071067811865476)
    hid = (pre * below).astype(BF16)
    slope = below + pre * (jnp.exp(pre * pre * -0.5) * 0.3989422804014327)
    low = (slope * units).astype(BF16)
    hidden[0] = hid
    grad_pre[0] = low
    out_acc[...] += dotf(hid, second)
    x_acc[...] += dotf(low, first, NT)

    @pl.when(step == 3)
    def _():
        result = out_acc[...]
        gate = gate_ref[:, :1]
        probs = probs_ref[...]
        grad_gate = jnp.sum(c[...].astype(F32) * result.astype(BF16).astype(F32), axis=1, keepdims=True)
        ids = lax.broadcasted_iota(jnp.int32, probs.shape, 1)
        mine = jnp.where(ids == own[0], 1.0, 0.0)
        logits = (grad_gate * probs * (mine - gate)).astype(BF16)
        grad_logits[...] = logits
        back[...] = (result * gate).astype(BF16)
        grad_x[...] = (x_acc[...] + dotf(logits, router[...], NT)).astype(BF16)


def run_expert(half, experts, own, x, c, shards, router, kept=()):
    rows, width = x.shape
    lanes = router.shape[1]
    whole = lambda u: (0, 0)
    anywhere = pl.BlockSpec(memory_space=pl.ANY)
    blocks = pl.BlockSpec((1, rows, width), lambda u: (u, half, 0))
    both = jax.ShapeDtypeStruct((4, 2 * rows, width), BF16)
    one = jax.ShapeDtypeStruct((rows, width), BF16)
    return pl.pallas_call(
        functools.partial(expert_kernel, experts, not kept),
        grid=(4,),
        in_specs=[
            pl.BlockSpec(memory_space=pltpu.SMEM),
            pl.BlockSpec((rows, width), whole),
            pl.BlockSpec((rows, width), whole),
        ]
        + [anywhere] * 4
        + [pl.BlockSpec((width, lanes), whole)]
        + [anywhere] * len(kept),
        out_specs=[blocks, blocks, pl.BlockSpec((rows, width), lambda u: (half, 0))]
        + [pl.BlockSpec((rows, width), whole)] * 2
        + [pl.BlockSpec((rows, lanes), whole)],
        out_shape=[both, both, jax.ShapeDtypeStruct((2 * rows, width), BF16), one, one]
        + [jax.ShapeDtypeStruct((rows, lanes), BF16)],
        scratch_shapes=[
            pltpu.VMEM((rows, 128), F32),
            pltpu.VMEM((rows, lanes), F32),
            pltpu.VMEM((rows, width), F32),
            pltpu.VMEM((rows, width), F32),
            pltpu.VMEM((4, width, width), BF16),
            pltpu.VMEM((4, width, width), BF16),
            pltpu.SemaphoreType.DMA((2, 4)),
        ],
        input_output_aliases={8 + i: i for i in range(len(kept))},
        compiler_params=pltpu.CompilerParams(
            dimension_semantics=("arbitrary",), vmem_limit_bytes=VMEM_LIMIT
        ),
        cost_estimate=BRIEF,
        name="run_expert",
    )(own, x, c, *shards, router, *kept)


def place_kernel(near, *refs):
    ours = pl.program_id(0) == 0
    zero_in, zero_out, one_in, one_out, two_in, two_out, three_in, three_out, out_in, out_out = refs
    pairs = (zero_in, one_in, two_in, three_in), (zero_out, one_out, two_out, three_out)
    for out, (zero, one, two, three) in zip((out_in, out_out), pairs):

        @pl.when(ours)
        def _():
            out[0] = zero[...].astype(F32) + one[...].astype(F32)

        @pl.when(jnp.logical_not(ours))
        def _():
            out[0] = two[...].astype(F32) + three[...].astype(F32)


def place_experts(near, blocks):
    width = blocks[0].shape[1]
    rows = 256
    steps = width // rows
    in_specs = []
    for u in range(4):
        for part in range(2):

            def index(i, r, near, u=u, part=part):
                own = r * (1 - i) + (steps - 1) * i if u < 2 else r * i
                return (part * steps + own, 0)

            in_specs.append(pl.BlockSpec((rows, width), index))
    out = pl.BlockSpec((1, rows, width), lambda i, r, near: (near[0] * (1 - i) + (1 - near[0]) * i, r, 0))
    return pl.pallas_call(
        place_kernel,
        grid_spec=pltpu.PrefetchScalarGridSpec(
            num_scalar_prefetch=1, grid=(2, steps), in_specs=in_specs, out_specs=[out, out]
        ),
        out_shape=[jax.ShapeDtypeStruct((2, width, width), F32)] * 2,
        compiler_params=pltpu.CompilerParams(
            dimension_semantics=("arbitrary", "arbitrary"), vmem_limit_bytes=VMEM_LIMIT
        ),
        cost_estimate=BRIEF,
        name="place_experts",
    )(jnp.reshape(near, (1,)), *[b for b in blocks for _ in range(2)])


def swap(x, bit):
    return lax.ppermute(x, "narrow", [(i, i ^ bit) for i in range(4)])


def swap_wide(x, bit):
    return lax.ppermute(x, "wide", [(i, i ^ bit) for i in range(lax.axis_size("wide"))])


def after(x, *others):
    return lax.optimization_barrier((x,) + others)[0]


def pick(x, index):
    return lax.dynamic_index_in_dim(x, index, 0, keepdims=False)


def scatter_first(blocks):
    half = blocks.shape[1] // 2
    return swap(blocks[3, :half], 1), swap(blocks[3, half:], 2)


def scatter_second(blocks, from_one, from_two):
    half = blocks.shape[1] // 2
    one = jnp.concatenate(
        (blocks[1, :half], (blocks[1, half:].astype(F32) + from_two.astype(F32)).astype(BF16)), axis=0
    )
    two = jnp.concatenate(
        ((blocks[2, :half].astype(F32) + from_one.astype(F32)).astype(BF16), blocks[2, half:]), axis=0
    )
    return swap(one, 1), swap(two, 2)


def sum_everywhere(x, beside):
    wide = lax.axis_index("wide")
    narrow = lax.axis_index("narrow")
    layers = lax.axis_size("wide") // 2
    rows = x.shape[0]
    x = jnp.pad(x.astype(BF16), ((0, -rows % (8 * layers)), (0, 0)))

    def layer_swap(a, k):
        return swap_wide(a, 2 * k)

    levels = ((2, wide % 2, swap_wide), (4, narrow, swap), (layers, wide // 2, layer_swap))
    for step, (count, place, send) in enumerate(levels):
        x = beside(step, x).reshape(count, x.shape[0] // count, -1)
        total = pick(x, place).astype(F32)
        for k in range(1, count):
            total = total + send(pick(x, place ^ k), k).astype(F32)
        x = total.astype(BF16)
    for step, (count, place, send) in enumerate(reversed(levels)):
        x = beside(3 + step, x)
        parts = jnp.stack([x] + [send(x, k) for k in range(1, count)])
        x = jnp.concatenate([pick(parts, place ^ i) for i in range(count)], axis=0)
    return x[:rows]


def on_device(
    hidden_in,
    lengths,
    routes,
    norm_gain_attn,
    query_weight,
    key_weight,
    value_weight,
    out_weight,
    bias_table,
    norm_gain_ffn,
    router_weight,
    expert_in,
    expert_out,
    cotangent,
):
    wide_count = lax.axis_size("wide")
    seq_count, rows, width = hidden_in.shape
    bucket_count, head_count = bias_table.shape
    pairs = width // 128
    tokens = seq_count * rows
    local_experts = expert_in.shape[0]
    expert_count = local_experts * wide_count
    capacity = 5 * tokens // (4 * expert_count)
    slots = wide_count * capacity
    me = lax.axis_index("narrow")
    near = me // 2
    far = 1 - near
    own = jnp.reshape(lax.axis_index("wide") * local_experts + near, (1,))

    source = hidden_in.astype(F32).reshape(tokens, width)
    factor_attn = rms_factor(source)
    normed = (source * factor_attn * norm_gain_attn).astype(BF16)
    normed_seqs = normed.reshape(seq_count, rows, width)
    queries = (dotf(normed, query_weight) * (LOG2E / 8)).astype(BF16).reshape(seq_count, rows, width)
    flags = neighbour_flags(me)
    klanes = key_lanes(me, lengths, rows)
    qlanes = query_lanes(bias_table, rows)
    tiles = bias_tiles(bias_table)
    router = jnp.pad(router_weight, ((0, 0), (0, -expert_count % 128)))
    shards = [
        jnp.concatenate((pick(expert_in, e), pick(expert_out, e)), axis=0) for e in (near, far)
    ]

    blocks = []
    for s in range(seq_count):
        mine = after(normed_seqs[s], *others) if s else normed_seqs[s]
        others = [swap(mine, u) for u in range(1, 4)]
        if s == 0:
            first = (others, queries, klanes, qlanes, tiles, shards)
            first = lax.optimization_barrier(first)
            first, queries, klanes, qlanes, tiles, shards = first
        blocks.append(jnp.stack([mine] + (others if s else first)))

    route = routes.reshape(tokens)
    position = me * rows + jnp.arange(rows, dtype=jnp.int32)
    live = (position[None, :] < lengths[:, None]).reshape(tokens)
    expert_ids = jnp.arange(expert_count, dtype=jnp.int32)
    chosen = ((route[:, None] == expert_ids[None, :]) & live[:, None]).astype(F32)
    token_ids = jnp.arange(tokens, dtype=jnp.int32)
    earlier = (token_ids[:, None] > token_ids[None, :]).astype(BF16)
    place = jnp.sum(dotf(earlier, chosen.astype(BF16)) * chosen, axis=-1).astype(jnp.int32)
    kept = live & (place < capacity)
    slot = route // local_experts * capacity + place
    slot_ids = jnp.arange(slots, dtype=jnp.int32)

    def slot_map(expert):
        due = jnp.where(kept & (route % local_experts == expert), slot, -1)
        return (slot_ids[:, None] == due[None, :]).astype(BF16)

    map_far, map_near = slot_map(far), slot_map(near)

    def exchange(values):
        sent = values.reshape(wide_count, -1, width)
        return lax.all_to_all(sent, "wide", 0, 0, tiled=True)

    cot = cotangent.reshape(tokens, width)
    cot_far = dotf(map_far, cot).astype(BF16).reshape(wide_count, capacity, width)
    cot_near = dotf(map_near, cot).astype(BF16).reshape(wide_count, capacity, width)
    got = exchange(jnp.concatenate((cot_far, cot_near), axis=1).reshape(2 * slots, width))
    cot_far = swap(got[:, :capacity].reshape(slots, width), 2)
    cot_near = got[:, capacity:].reshape(slots, width)

    kvs, atts, qaugs = [], [], []
    for s in range(seq_count):
        rows_all = blocks[s].reshape(4 * rows, width)
        kvs.append(
            [
                dotf(rows_all, w).astype(BF16).reshape(1, 4, rows, width)
                for w in (key_weight, value_weight)
            ]
        )
        cost = LONG if s == 0 else BRIEF
        att, qaug = attend_forward(s, cost, flags, queries, *kvs[s], klanes, qlanes, tiles)
        atts.append(att)
        qaugs.append(qaug)
        if s == 0:
            shards, _ = lax.optimization_barrier((shards, att))
            shards = [shards[0], swap(shards[0], 1), swap(shards[1], 2)]
    attended = jnp.concatenate(atts, axis=0).reshape(tokens, width)
    attended, shards = lax.optimization_barrier((attended, shards))
    shards.append(swap(shards[2], 1))
    residual = source + dotf(attended, out_weight)
    factor_ffn = rms_factor(residual)
    ffn_input = (residual * factor_ffn * norm_gain_ffn).astype(BF16)

    sent_far = dotf(map_far, ffn_input).astype(BF16)
    sent_near = dotf(map_near, after(ffn_input, sent_far)).astype(BF16)
    x_far = swap(exchange(sent_far).reshape(slots, width), 2)
    x_near = exchange(sent_near).reshape(slots, width)
    *shared, back_far, grad_x_far, logits_far = run_expert(
        0, expert_count, own, x_far, cot_far, shards, router
    )
    grad_x_far = swap(grad_x_far, 2)
    hidden, grad_pre, low_c, back_near, grad_x_near, logits_near = run_expert(
        1, expert_count, own, x_near, cot_near, shards, router, tuple(shared)
    )
    sent = jnp.concatenate(
        [x.reshape(wide_count, capacity, width) for x in (grad_x_far, grad_x_near)], axis=1
    )
    got = exchange(sent)

    x_far, x_near, low_c, logits_far, logits_near, _ = lax.optimization_barrier(
        (x_far, x_near, low_c, logits_far, logits_near, sent)
    )
    xs = jnp.concatenate((x_far, x_near), axis=0)
    grad_experts = [None] * 4
    for u in (3, 1, 2, 0):
        both = (dotf(xs, grad_pre[u], TN), dotf(hidden[u], low_c, TN))
        both = jnp.concatenate([x.astype(BF16) for x in both], axis=0)
        grad_experts[u] = swap(both, u) if u else both
    back_far = swap(after(back_far, sent), 2)
    got, grad_experts[0] = lax.optimization_barrier((got, grad_experts[0]))
    grad_x_far, grad_x_near = (
        x.reshape(slots, width) for x in (got[:, :capacity], got[:, capacity:])
    )

    grad_router = dotf(x_far, logits_far, TN) + dotf(x_near, logits_near, TN)

    grad_ffn_input = dotf(map_near, grad_x_near, TN) + dotf(map_far, grad_x_far, TN)
    grad_norm, gain_ffn = rms_pull(residual, factor_ffn, norm_gain_ffn, grad_ffn_input)
    gain_ffn = jnp.sum(gain_ffn, axis=0)
    grad_residual = cot.astype(F32) + grad_norm
    grad_branch = grad_residual.astype(BF16)
    grad_out_weight = dotf(attended, grad_branch, TN)
    grad_attended = dotf(grad_branch, out_weight, NT).astype(BF16).reshape(seq_count, rows, width)
    back = jnp.concatenate(
        [x.reshape(wide_count, capacity, width) for x in (back_far, back_near)], axis=1
    )
    grad_attended, back = lax.optimization_barrier((grad_attended, back))
    back = exchange(back)
    def normed_blocks(s):
        part = dotf(dks[s], key_weight, NT) + dotf(dvs[s], value_weight, NT)
        return part.astype(BF16).reshape(4, rows, width)

    dqs, dks, dvs = [], [], []
    table = 0.0
    for s in range(seq_count):
        dq, dk, dv, table_one = attend_backward(
            s, flags, qaugs[s], *kvs[s], atts[s], grad_attended, klanes, tiles
        )
        dqs.append(dq.reshape(rows, width))
        dks.append(dk.reshape(4 * rows, width))
        dvs.append(dv.reshape(4 * rows, width))
        table = table + table_one[0]
        if s == 0:
            parts = normed_blocks(0)
            grad_attended, parts = lax.optimization_barrier((grad_attended, parts))
            halves = scatter_first(parts)
    dqs, dks, dvs, grad_experts, back, halves = lax.optimization_barrier(
        (dqs, dks, dvs, grad_experts, back, halves)
    )
    scattered = [scatter_second(parts, *halves)]
    ours = [parts[0]]
    summands = [
        sum(dotf(x.reshape(-1, width), g, TN) for x, g in zip(xs, grads))
        for xs, grads in ((normed_seqs, dqs), (blocks, dks), (blocks, dvs))
    ]
    table = table_grad(table, rows, bucket_count)
    rest = jnp.concatenate(
        (
            jnp.pad(table, ((0, 0), (0, width - head_count))),
            grad_router.T[:expert_count],
            gain_ffn[None],
            jnp.zeros((-(bucket_count + expert_count + 1) % 64, width), F32),
        ),
        axis=0,
    )
    summands = [x.astype(BF16) for x in summands + [grad_out_weight, rest]]
    summands, dqs, dks, dvs = lax.optimization_barrier((summands, dqs, dks, dvs))

    def beside(step, x):
        nonlocal halves, back
        if step == 1:
            ours.append(normed_blocks(1))
            x, ours[1], scattered[0] = lax.optimization_barrier((x, ours[1], scattered[0]))
            halves = scatter_first(ours[1])
        if step == 2:
            x, halves = lax.optimization_barrier((x, halves))
            scattered.append(scatter_second(ours[1], *halves))
            ours[1] = ours[1][0]
        if step == 4:
            x, scattered[1], back = lax.optimization_barrier((x, scattered[1], back))
        return x

    sums = sum_everywhere(jnp.concatenate(summands, axis=0), beside).astype(F32)
    block_out = residual + dotf(map_far, back[:, :capacity].reshape(slots, width), TN)
    block_out = block_out + dotf(map_near, back[:, capacity:].reshape(slots, width), TN)
    grad_in, grad_out = place_experts(near, grad_experts)
    grad_normed = jnp.concatenate(
        [
            mine.astype(F32) + sum(x.astype(F32) for x in arrived) + dotf(dq, query_weight, NT)
            for mine, arrived, dq in zip(ours, scattered, dqs)
        ],
        axis=0,
    )
    grad_hidden = grad_residual + rms_pull(source, factor_attn, norm_gain_attn, grad_normed)[0]

    sum_q, sum_k, sum_v, sum_out = (sums[i * width : (i + 1) * width] for i in range(4))
    sum_rest = sums[4 * width :]
    sum_router = sum_rest[bucket_count : bucket_count + expert_count]
    gain_attn = jnp.sum(
        sum_q * query_weight.astype(F32)
        + sum_k * key_weight.astype(F32)
        + sum_v * value_weight.astype(F32),
        axis=1,
    )
    out_shape = (seq_count, rows, width)
    return (
        block_out.reshape(out_shape),
        grad_hidden.reshape(out_shape),
        gain_attn / norm_gain_attn,
        sum_q,
        sum_k,
        sum_v,
        sum_out,
        sum_rest[:bucket_count, :head_count],
        sum_rest[bucket_count + expert_count],
        sum_router.T,
        grad_in,
        grad_out,
    )


def solution(mesh):
    placed = (
        P("wide", "narrow", None),
        P("wide"),
        P("wide", "narrow", None),
        P(),
        P(),
        P(),
        P(),
        P(),
        P(),
        P(),
        P(),
        P("wide", None, "narrow"),
        P("wide", "narrow", None),
        P("wide", "narrow", None),
    )
    return jax.shard_map(
        on_device,
        mesh=mesh,
        in_specs=placed,
        out_specs=(
            P("wide", "narrow", None),
            P("wide", "narrow", None),
            P(),
            P(),
            P(),
            P(),
            P(),
            P(),
            P(),
            P(),
            P("wide", None, "narrow"),
            P("wide", "narrow", None),
        ),
        check_vma=False,
    )
```
